256 devices in a mesh: dp: 16 (over x_lo, z), tensor: 4 (over x_hi, core), latent: 4 (over y).
Axes of the slice: x: 4 (x_hi: 2, x_lo: 2; x = x_hi * 2 + x_lo), y: 4, z: 8, core: 2. Of those that a mesh axis runs over, the one named last changes fastest.
Arguments:
- residual: bfloat16 [2048, 4608], P('dp', ('tensor', 'latent')), may hold values from -6 to 6
- segments: int32 [16, 128], P('dp'), may hold values from 0 to 3, never falling along the last dimension, each value on 1 to 64 neighbouring positions
- row_perm: int32 [2048], P('dp'), may hold values from 0 to 2047, as said below
- pre_gain: float32 [4608], replicated, may hold values from 0.25 to 1.75
- post_gain: float32 [4608], replicated, may hold values from 0.25 to 1.75
- w_query: bfloat16 [4608, 4096], P(None, ('tensor', 'latent')), may hold values from -0.70710678 to 0.70710678
- w_key: bfloat16 [4608, 2048], P(None, ('tensor', 'latent')), may hold values from -0.09375 to 0.09375
- w_value: bfloat16 [4608, 2048], P(None, ('tensor', 'latent')), may hold values from -0.09375 to 0.09375
- w_out: bfloat16 [4096, 4608], P(('tensor', 'latent')), may hold values from -0.09375 to 0.09375
- sae_weight: bfloat16 [4608, 16384], P('dp', ('tensor', 'latent')), may hold values from -0.09375 to 0.09375
- enc_bias: float32 [16384], P(('tensor', 'latent')), may hold values from -3 to 3
- thresholds: float32 [16384], P(('tensor', 'latent')), may hold values from 0.2 to 1.2
- dec_bias: float32 [4608], replicated, may hold values from -3 to 3
Outputs:
- weight_grad: bfloat16 [4608, 16384], P('dp', ('tensor', 'latent'))
- bias_grad: float32 [16384], P(('tensor', 'latent'))
- codes: bfloat16 [2048, 16384], P('dp', ('tensor', 'latent'))
The draws below stay inside these ranges and needn't reach their ends.
Inputs may be any that keep to these rules, and one draw needn't show every extreme that they name: `segments`: segment numbers never fall along a row. row_perm is a permutation. Within the rows 128 g to 128 (g + 1) - 1, the 8 rows starting at 128 g + s * 8 hold only indices from 128 s to 128 (s + 1) - 1.
All inputs are finite; a program needn't handle non-finite values.
Results may differ from the reference program's by a relative error of at most 0.03.
Values may be sent and summed in bfloat16 or wider, within the bound.
A program may use at most 128 MiB of HBM per device.

```python
import math
import jax
import jax.numpy as jnp
import numpy as np
from jax import lax

D = 4608
HEADS = 32
KV_HEADS = 16
HEAD = 128
LATENTS = 16384
TOK_G = 128
GROUPS = 16
TOKENS = 2048
BLOCK = 8


def draw_row_perm(key, part):
    keys = jax.random.split(key, GROUPS)
    orders = jax.vmap(lambda single_key: jax.random.permutation(single_key, TOK_G))(keys)
    orders = orders.astype(jnp.int32).reshape(GROUPS, GROUPS, BLOCK)
    orders = orders + (jnp.arange(GROUPS, dtype=jnp.int32) * TOK_G)[:, None, None]
    return jnp.transpose(orders, (1, 0, 2)).reshape(TOKENS).astype(jnp.int32)


def draw_w_query(key, part):
    head_key, entry_key = jax.random.split(jax.random.fold_in(key, 11))
    head_scale = jnp.exp(jax.random.uniform(head_key, (HEADS,), jnp.float32, 0.0, math.log(12.0)))
    entries = jnp.clip(jax.random.normal(entry_key, (D, HEADS, HEAD), jnp.float32), -4.0, 4.0)
    weight = entries * head_scale[None, :, None] * D ** (-0.5)
    return weight.reshape(D, HEADS * HEAD).astype(jnp.bfloat16)


def level_of(stream_key, shape, shards, least, largest):
    level = 1.0
    for dim, parts in shards:
        steps = jax.random.uniform(jax.random.fold_in(jax.random.fold_in(stream_key, 6), dim), (parts,), jnp.float32, least / len(shards), largest / len(shards))
        level = level * jnp.repeat(jnp.exp(steps), shape[dim] // parts).reshape((-1,) + (1,) * (len(shape) - 1 - dim))
    return level


def length_profile(number_of, total, limit, lean):
    portions = [(1 << 20) // math.isqrt(rank ** lean) + 1 for rank in range(2, number_of + 1)]
    rest, holding = total - limit - (number_of - 1), [1] * (number_of - 1)
    while rest > 0:
        movable = [i for i in range(number_of - 1) if holding[i] < limit]
        pool, left = sum([portions[i] for i in movable]), rest
        for i in movable:
            extra = min(limit - holding[i], max(1, left * portions[i] // pool), rest)
            holding[i] = holding[i] + extra
            rest = rest - extra
    return np.array([limit] + holding)


def ragged_sizes(rng, amount, total, reach, skew):
    if amount == 2:
        one = jax.random.randint(rng, (), max(1, total - reach), min(reach, total - 1) + 1)
        return jnp.stack([one, total - one])
    sizes = jnp.asarray(length_profile(amount, total, reach, skew), jnp.int32)
    twos = (amount - 1) // 2
    source_of, sink = sizes[1:1 + 2 * twos:2], sizes[2:2 + 2 * twos:2]
    margin = jnp.minimum(source_of - 1, reach - sink)
    moved = jax.random.randint(jax.random.fold_in(rng, 1), (twos,), 0, 1 << 20) % (margin + 1)
    sizes = sizes.at[1:1 + 2 * twos:2].set(source_of - moved).at[2:2 + 2 * twos:2].set(sink + moved)
    return sizes[jax.random.permutation(jax.random.fold_in(rng, 2), amount)]


def centred(own_key, dims, deviation, reach, cuts=(), kind=jnp.bfloat16):
    values = deviation * jax.random.normal(own_key, dims, jnp.float32)
    if cuts:
        values = values * level_of(own_key, dims, cuts, -0.22, 0.18)
    return jnp.clip(values, -reach, reach).astype(kind)


def setup_inputs(seed: int = 0) -> dict:
    arg_keys = jax.random.split(jax.random.key(seed), 14)
    return {
        "residual": centred(arg_keys[0], (TOKENS, D), 1.0, 6.0, ((0, 16), (1, 16))),
        "segments": jax.vmap(lambda own: jnp.searchsorted(jnp.cumsum(ragged_sizes(own, 4, TOK_G, TOK_G // 2, 0)), jnp.arange(TOK_G), side="right"))(jax.random.split(arg_keys[1], GROUPS)).reshape((GROUPS, TOK_G)).astype(jnp.int32),
        "row_perm": draw_row_perm(jax.random.fold_in(arg_keys[13], 71), 0),
        "pre_gain": jnp.clip(1.0 + 0.15 * jax.random.normal(arg_keys[3], (D,), jnp.float32), 0.25, 1.75),
        "post_gain": jnp.clip(1.0 + 0.15 * jax.random.normal(arg_keys[4], (D,), jnp.float32), 0.25, 1.75),
        "w_query": draw_w_query(jax.random.fold_in(arg_keys[13], 71), 0),
        "w_key": centred(arg_keys[6], (D, KV_HEADS * HEAD), D ** -0.5, 0.09375, ((1, 16),)),
        "w_value": centred(arg_keys[7], (D, KV_HEADS * HEAD), D ** -0.5, 0.09375, ((1, 16),)),
        "w_out": centred(arg_keys[8], (HEADS * HEAD, D), (HEADS * HEAD) ** -0.5, 0.09375, ((0, 16),)),
        "sae_weight": centred(arg_keys[9], (D, LATENTS), D ** -0.5, 0.09375, ((0, 16), (1, 16))),
        "enc_bias": centred(arg_keys[10], (LATENTS,), 0.5, 3.0, ((0, 16),), jnp.float32),
        "thresholds": jnp.clip(0.2 + 1 * jax.random.uniform(arg_keys[11], (LATENTS,), jnp.float32) ** level_of(arg_keys[11], (LATENTS,), ((0, 16),), -0.2, 0.2), 0.2, 1.2),
        "dec_bias": centred(arg_keys[12], (D,), 0.5, 3.0, (), jnp.float32),
    }


epsilon = 1e-06
softcap = 50.0
ramp_width = 0.05
rotary_base = 10000.0

def rms_scale(field, gain_vec):
    return field * lax.rsqrt(lax.optimization_barrier(jnp.mean(field * field, axis=-1, keepdims=True)) + epsilon) * gain_vec

def rotate(field, positions):
    half_width = field.shape[-1] // 2
    frequency = rotary_base ** (-2.0 * jnp.arange(half_width, dtype=jnp.float32) / field.shape[-1])
    angles = positions[..., :, None, None] * frequency
    cosine = jnp.cos(angles)
    sine_part = jnp.sin(angles)
    first_half = field[..., :half_width]
    second_half = field[..., half_width:]
    return jnp.concatenate([first_half * cosine - second_half * sine_part, second_half * cosine + first_half * sine_part], axis=-1)

def doc_masks(segment_ids):
    same_doc = segment_ids[..., :, None] == segment_ids[..., None, :]
    indices = jnp.arange(segment_ids.shape[-1], dtype=jnp.int32)
    earlier = indices[None, :] < indices[:, None]
    positions = lax.optimization_barrier(jnp.sum((same_doc & earlier).astype(jnp.float32), axis=-1))
    attend_mask = (same_doc & (indices[None, :] <= indices[:, None])).astype(jnp.float32)
    return (positions, attend_mask)

def reference(residual, segments, row_perm, pre_gain, post_gain, w_query, w_key, w_value, w_out, sae_weight, enc_bias, thresholds, dec_bias):
    stream = residual.astype(jnp.float32)
    normed = rms_scale(stream, pre_gain).astype(jnp.bfloat16)
    positions, attend_mask = doc_masks(segments)
    group_ratio = HEADS // KV_HEADS
    query_projected = jnp.dot(normed, w_query, preferred_element_type=jnp.float32).reshape(GROUPS, TOK_G, HEADS, HEAD)
    query_projected = rotate(query_projected, positions).astype(jnp.bfloat16).reshape(GROUPS, TOK_G, KV_HEADS, group_ratio, HEAD)
    key_projected = jnp.dot(normed, w_key, preferred_element_type=jnp.float32).reshape(GROUPS, TOK_G, KV_HEADS, HEAD)
    key_projected = rotate(key_projected, positions).astype(jnp.bfloat16)
    value_projected = jnp.dot(normed, w_value, preferred_element_type=jnp.float32).astype(jnp.bfloat16).reshape(GROUPS, TOK_G, KV_HEADS, HEAD)
    logit_matrix = jnp.einsum('btgrd,bsgd->bgrts', query_projected.astype(jnp.float32), key_projected.astype(jnp.float32)) * (D / HEADS) ** (-0.5)
    logit_matrix = softcap * jnp.tanh(logit_matrix / softcap)
    weighted = jnp.exp(logit_matrix) * attend_mask[:, None, None]
    attention_weights = (weighted / lax.optimization_barrier(jnp.sum(weighted, axis=-1, keepdims=True))).astype(jnp.bfloat16)
    head_out = jnp.einsum('bgrts,bsgd->btgrd', attention_weights.astype(jnp.float32), value_projected.astype(jnp.float32))
    head_out = head_out.astype(jnp.bfloat16).reshape(TOKENS, HEADS * HEAD)
    attn_out = jnp.dot(head_out, w_out, preferred_element_type=jnp.float32)
    hidden = (stream + rms_scale(attn_out, post_gain)).astype(jnp.bfloat16)
    sae_rows = hidden[row_perm]
    pre_acts = jnp.dot(sae_rows, sae_weight, preferred_element_type=jnp.float32) + enc_bias
    open_gate = jax.nn.sigmoid((pre_acts - thresholds) / ramp_width)
    latent_acts = (pre_acts * open_gate).astype(jnp.bfloat16)
    contract_last = (((1,), (1,)), ((), ()))
    rebuilt = lax.dot_general(latent_acts, sae_weight, contract_last, preferred_element_type=jnp.float32)
    error_bf = (rebuilt + dec_bias - sae_rows.astype(jnp.float32)).astype(jnp.bfloat16)
    latent_gradient = jnp.dot(error_bf, sae_weight, preferred_element_type=jnp.float32)
    slope = open_gate + pre_acts * open_gate * (1.0 - open_gate) / ramp_width
    grad_pre = (latent_gradient * slope).astype(jnp.bfloat16)
    grad_scale = TOKENS ** (-0.5)
    contract_first = (((0,), (0,)), ((), ()))

    def add_group(running, group_items):
        rows_part, error_part, grad_part, acts_part = group_items
        group_term = lax.dot_general(rows_part, grad_part, contract_first, preferred_element_type=jnp.float32)
        group_term = group_term + lax.dot_general(error_part, acts_part, contract_first, preferred_element_type=jnp.float32)
        rounded = lax.optimization_barrier((grad_scale * group_term).astype(jnp.bfloat16))
        return (running + rounded.astype(jnp.float32), None)
    group_items = (sae_rows.reshape(GROUPS, TOK_G, D), error_bf.reshape(GROUPS, TOK_G, D), grad_pre.reshape(GROUPS, TOK_G, LATENTS), latent_acts.reshape(GROUPS, TOK_G, LATENTS))
    running, _ = lax.scan(add_group, jnp.zeros((D, LATENTS), jnp.float32), group_items)
    weight_grad = running.astype(jnp.bfloat16)
    bias_grad = grad_scale * lax.optimization_barrier(jnp.sum(grad_pre.astype(jnp.float32), axis=0))
    return (weight_grad, bias_grad, latent_acts)
```

```python
import math

import jax
import jax.numpy as jnp
from jax import lax
from jax.experimental import pallas as pl
from jax.experimental.pallas import tpu as pltpu
from jax.sharding import PartitionSpec as P

D = 4608
HEADS = 32
HEAD = 128
LANES = 1024
TOK = 128
GROUPS = 16
TOKENS = TOK * GROUPS
BLOCK = 8
WIDTH = D // 16
SEMS = 300

epsilon = 1e-06
softcap = 50.0
ramp_width = 0.05
rotary_base = 10000.0

MESH = pl.DeviceIdType.MESH
F32 = jnp.float32
BF16 = jnp.bfloat16
ROW_BY_ROW = (((1,), (1,)), ((), ()))


def dot(a, b):
    return jnp.dot(a, b, preferred_element_type=F32)


def dot_t(a, b):
    return lax.dot_general(a, b, ROW_BY_ROW, preferred_element_type=F32)


class Place:
    def __init__(self):
        self.dp = lax.axis_index("dp")
        self.ten = lax.axis_index("tensor")
        self.lat = lax.axis_index("latent")
        self.xl, self.z = self.dp // 8, self.dp % 8
        self.xh, self.core = self.ten // 2, self.ten % 2
        self.t = self.ten * 4 + self.lat

    def at(self, dp=None, ten=None, lat=None):
        return {
            "dp": self.dp if dp is None else dp,
            "tensor": self.ten if ten is None else ten,
            "latent": self.lat if lat is None else lat,
        }

    def chip(self, k, sign=1):
        return (self.xh + k // 4) % 2, (self.lat + sign * (k % 4) + 4) % 4

    def piece(self, k, core, sign=1):
        xh, y = self.chip(k, sign)
        return (xh * 2 + core) * 4 + y

    def peer(self, k, core=None):
        xh, y = self.chip(k)
        return self.at(ten=xh * 2 + (self.core if core is None else core), lat=y)

    def sibling(self):
        return self.at(ten=self.xh * 2 + 1 - self.core)


class Net:
    def __init__(self, send, recv):
        self.send, self.recv, self.used, self.open = send, recv, 0, []

    def copy(self, src, dst, device):
        i = self.used
        self.used += 1
        assert i < SEMS
        c = pltpu.make_async_remote_copy(
            src_ref=src,
            dst_ref=dst,
            send_sem=self.send.at[i],
            recv_sem=self.recv.at[i],
            device_id=device,
            device_id_type=MESH,
        )
        self.open.append(c)
        return c

    def close(self):
        for c in self.open:
            c.wait_send()
        self.open = []


FAR_FIRST = (6, 5, 7, 4, 2, 1, 3)
NEAR_FIRST = (1, 3, 2, 4, 5, 7, 6)


class Gather:
    def __init__(self, net, me, buf):
        self.net, self.me, self.buf = net, me, buf

    def rows(self, index):
        return self.buf.at[pl.ds(pl.multiple_of(index * WIDTH, 32), WIDTH)]

    def start(self):
        me, own = self.me, self.rows(self.me.t)
        self.far = {}
        for k in FAR_FIRST:
            self.far[k] = self.net.copy(own, own, me.peer(k))
            self.far[k].start()
        self.near = {0: self.net.copy(own, own, me.sibling())}
        self.near[0].start()

    def finish(self):
        me = self.me
        for k in NEAR_FIRST:
            self.far[k].wait_recv()
            got = self.rows(me.piece(k, me.core, -1))
            self.near[k] = self.net.copy(got, got, me.sibling())
            self.near[k].start()
        for k in (0, *NEAR_FIRST):
            self.near[k].wait_recv()


def reduce_to_owner(net, me, part, mate, out, got):
    def rows(ref, index):
        return ref.at[pl.ds(pl.multiple_of(index * WIDTH, 32), WIDTH)]

    order = (*FAR_FIRST, 0)
    pair = {}
    for k in order:
        pair[k] = net.copy(rows(part, me.piece(k, 1 - me.core)), mate.at[k], me.sibling())
        pair[k].start()
    away = {}
    for k in order:
        pair[k].wait_recv()
        both = rows(part, me.piece(k, me.core))[...].astype(F32) + mate[k].astype(F32)
        if k == 0:
            total = both
        else:
            out[k] = both.astype(BF16)
            away[k] = net.copy(out.at[k], got.at[k], me.peer(k))
            away[k].start()
    for k in NEAR_FIRST:
        away[k].wait_recv()
        total = total + got[k].astype(F32)
    return total


class Ring:
    def __init__(self, net, me, buf, size, cut, half_a, half_b):
        self.net, self.me, self.buf, self.size = net, me, buf, size
        self.parts = {
            "a": (me.xl, 0, cut, half_a),
            "b": (me.xl, cut, size - cut, half_b),
            "c": (1 - me.xl, cut, size - cut, half_b),
        }
        self.moves, self.cross = {}, {}

    def rows(self, block, lo, count):
        return self.buf.at[pl.ds(pl.multiple_of(block * self.size + lo, 16), count)]

    def range(self, part, sign, step):
        _, lo, count, half = self.parts[part]
        if step < 4:
            return lo, count
        return (lo, half) if sign > 0 else (lo + half, count - half)

    def move(self, part, sign, step):
        me = self.me
        lo, count = self.range(part, sign, step)
        block = self.parts[part][0] * 8 + (me.z - sign * (step - 1) + 8) % 8
        ref = self.rows(block, lo, count)
        c = self.net.copy(ref, ref, me.at(dp=me.xl * 8 + (me.z + sign + 8) % 8))
        c.start()
        self.moves[part, sign, step] = c

    def over(self, name, block, lo, count):
        me = self.me
        ref = self.rows(block, lo, count)
        c = self.net.copy(ref, ref, me.at(dp=(1 - me.xl) * 8 + me.z))
        c.start()
        self.cross[name] = c

    def start(self):
        _, lo, count, _ = self.parts["b"]
        self.over("b", self.me.dp, lo, count)
        for part in "ab":
            for sign in (1, -1):
                self.move(part, sign, 1)
        _, lo, count, _ = self.parts["a"]
        self.over("a", self.me.dp, lo, count)

    def tick(self, step):
        if step == 0:
            self.cross["b"].wait_recv()
            for sign in (1, -1):
                self.move("c", sign, 1)
            return
        for part in "abc":
            for sign in (1, -1):
                self.moves[part, sign, step].wait_recv()
                if step < 4:
                    self.move(part, sign, step + 1)
                if part == "a":
                    lo, count = self.range(part, sign, step)
                    block = self.me.xl * 8 + (self.me.z - sign * step + 8) % 8
                    self.over((sign, step), block, lo, count)

    def crossed(self):
        for name, c in self.cross.items():
            if name != "b":
                c.wait_recv()


def transpose_into(src, dst):
    @pl.loop(0, D // TOK)
    def _(i):
        at = pl.multiple_of(i * TOK, TOK)
        dst[:, pl.ds(at, TOK)] = src[pl.ds(at, TOK), :].T


def body(
    res,
    seg,
    perm,
    pre_gain,
    gain_col,
    wq_hbm,
    wk_hbm,
    wv_hbm,
    wo_hbm,
    w_hbm,
    enc_bias,
    thr,
    bias_col,
    wg_out,
    bg_out,
    codes_out,
    wq,
    wk,
    wv,
    wo,
    w,
    feat,
    rows,
    part,
    mate,
    out,
    got,
    part2,
    mate2,
    out2,
    got2,
    asked,
    squares,
    sent,
    taken,
    sae_f,
    err_f,
    sae_mine,
    err_mine,
    turned_s,
    turned_e,
    sae_t,
    err_t,
    pre,
    gate,
    codes,
    grads,
    wg,
    final,
    bg,
    local_sem,
    send_sem,
    recv_sem,
):
    me = Place()
    net = Net(send_sem, recv_sem)

    loads = []
    for i, (src, dst) in enumerate(
        [
            (w_hbm, w.at[pl.ds(pl.multiple_of(me.dp * WIDTH, 32), WIDTH)]),
            (wq_hbm, wq),
            (wk_hbm, wk),
            (wv_hbm, wv),
            (wo_hbm, wo),
        ]
    ):
        loads.append(pltpu.make_async_copy(src, dst, local_sem.at[i]))
        loads[-1].start()

    turn_to = me.at(dp=me.t, ten=((me.dp + 1) % 16) // 4, lat=((me.dp + 1) % 16) % 4)
    before = (me.t + 15) % 16
    turn_from = me.at(dp=before, ten=me.dp // 4, lat=me.dp % 4)

    barrier = pltpu.get_barrier_semaphore()
    greeted = [turn_from]
    for k in range(8):
        for core in range(2):
            if k == 0:
                continue
            greeted.append(me.peer(k, core))
    greeted.append(me.sibling())

    def dp_peer(j):
        return ((me.xl + j // 8) % 2) * 8 + (me.z + j % 8) % 8

    for j in range(1, 16):
        greeted.append(me.at(dp=dp_peer(j)))
    for device in greeted:
        pl.semaphore_signal(barrier, inc=1, device_id=device, device_id_type=MESH)
    pl.semaphore_wait(barrier, len(greeted))

    feat[pl.ds(pl.multiple_of(me.t * WIDTH, 32), WIDTH), :] = res[...]
    gather = Gather(net, me, feat)
    gather.start()

    def asked_rows(index):
        return asked.at[pl.ds(pl.multiple_of(index * 8, 8), 8)]

    asked_rows(me.dp)[...] = jnp.broadcast_to(perm[...], (8, TOK))
    asks = []
    for j in range(1, 16):
        asks.append(net.copy(asked_rows(me.dp), asked_rows(me.dp), me.at(dp=dp_peer(j))))
        asks[-1].start()

    loads[0].wait()
    ring = Ring(net, me, w, WIDTH, 176, 96, 48)
    ring.start()

    lane = lax.broadcasted_iota(jnp.int32, (TOK, TOK), 1)
    row = lax.broadcasted_iota(jnp.int32, (TOK, TOK), 0)
    seg_k = jnp.broadcast_to(seg[...].astype(F32), (TOK, TOK))
    same = seg_k == seg_k.T
    position = jnp.sum(jnp.where(same & (lane < row), 1.0, 0.0), axis=1, keepdims=True)
    allowed = same & (lane <= row)
    step = (lane % 64).astype(F32)
    angle = position * jnp.exp(step * (-2.0 / HEAD * math.log(rotary_base)))
    cosine = jnp.cos(angle)
    sine = jnp.sin(angle)
    sine = jnp.where(lane < 64, -sine, sine)

    for c in asks:
        c.wait_recv()
    place = 8 * me.dp + row % 8
    mine = jnp.where(lane == place, asked[...], 0).astype(F32)
    number = jnp.sum(mine, axis=1, keepdims=True) - (me.dp * TOK).astype(F32)
    pick = jnp.where(number == lane.astype(F32), 1.0, 0.0).astype(BF16)

    gather.finish()
    ring.tick(0)
    transpose_into(feat, rows)

    def add_squares(i, acc):
        x = rows[:, pl.ds(pl.multiple_of(i * TOK, TOK), TOK)].astype(F32)
        return acc + x * x

    acc = lax.fori_loop(0, D // TOK, add_squares, jnp.zeros((TOK, TOK), F32), unroll=4)
    scale = lax.rsqrt(jnp.sum(acc, axis=1, keepdims=True) * (1.0 / D) + epsilon)

    @pl.loop(0, D // TOK, unroll=4)
    def _(i):
        at = pl.ds(pl.multiple_of(i * TOK, TOK), TOK)
        rows[:, at] = (rows[:, at].astype(F32) * scale * pre_gain[:, at]).astype(BF16)

    for c in loads[1:]:
        c.wait()
    normed = rows[...]
    query = dot(normed, wq[...])
    key = dot(normed, wk[...])
    value = dot(normed, wv[...]).astype(BF16)

    def rotate(v):
        return (v * cosine + pltpu.roll(v, 64, 1) * sine).astype(BF16)

    key = rotate(key)
    heads = []
    for h in range(2):
        q = rotate(query[:, h * HEAD : (h + 1) * HEAD])
        scores = dot_t(q, key) * (D / HEADS) ** (-0.5)
        scores = softcap * jnp.tanh(scores / softcap)
        weighted = jnp.where(allowed, jnp.exp(scores), 0.0)
        probs = (weighted / jnp.sum(weighted, axis=1, keepdims=True)).astype(BF16)
        heads.append(dot(probs, value).astype(BF16))
    heads = jnp.concatenate(heads, axis=1)

    ring.tick(1)

    @pl.loop(0, D // 256)
    def _(i):
        at = pl.multiple_of(i * 256, 256)
        part[pl.ds(at, 256), :] = dot(heads, wo[:, pl.ds(at, 256)]).astype(BF16).T

    attn = reduce_to_owner(net, me, part, mate, out, got)

    def square_rows(index):
        return squares.at[pl.ds(pl.multiple_of(index * 8, 8), 8)]

    own = jnp.sum(attn * attn, axis=0, keepdims=True)
    square_rows(me.t)[...] = jnp.broadcast_to(own, (8, TOK))
    sums = []
    for k in range(8):
        for core in range(2):
            if k == 0 and core == 0:
                continue
            device = me.peer(k, (me.core + core) % 2)
            sums.append(net.copy(square_rows(me.t), square_rows(me.t), device))
            sums[-1].start()
    ring.tick(2)
    for c in sums:
        c.wait_recv()
    total = jnp.sum(squares[...], axis=0, keepdims=True) * (0.125 / D)
    hidden = res[...].astype(F32) + attn * lax.rsqrt(total + epsilon) * gain_col[...]
    hidden = hidden.astype(BF16)

    low = dot_t(pick, hidden[:256])
    high = dot_t(pick, hidden[32:])
    for g in range(GROUPS):
        block = jnp.concatenate([low[8 * g : 8 * g + 8], high[8 * g : 8 * g + 8]], axis=0)
        sent[g] = block.astype(BF16)
    taken[me.dp] = sent[me.dp]
    moves = []
    for j in range(1, 16):
        to = dp_peer(j)
        moves.append(net.copy(sent.at[to], taken.at[me.dp], me.at(dp=to)))
        moves[-1].start()
    for c in moves:
        c.wait_recv()
    low, high = [], []
    for g in range(GROUPS):
        block = taken[g].astype(F32)
        low.append(block[:8])
        high.append(block[8:, 128:])
    low = jnp.concatenate(low, axis=0)
    high = jnp.concatenate(high, axis=0)
    sae_part = jnp.concatenate([low.T, high.T[96:]], axis=0)
    sae_mine[...] = sae_part.astype(BF16)

    def feature_rows(ref, index):
        return ref.at[pl.ds(pl.multiple_of(index * WIDTH, 32), WIDTH)]

    feature_rows(sae_f, me.t)[...] = sae_mine[...]
    gather = Gather(net, me, sae_f)
    gather.start()
    turn_s = net.copy(sae_mine, turned_s, turn_to)
    turn_s.start()
    gather.finish()
    ring.tick(3)
    transpose_into(sae_f, rows)
    turn_s.wait_recv()
    feature_rows(sae_t, me.t)[...] = turned_s[...]
    gather_st = Gather(net, me, sae_t)
    gather_st.start()
    ring.tick(4)
    ring.crossed()

    ring_c = Ring(net, me, codes, TOK, 80, 48, 32)
    my_rows = pl.ds(pl.multiple_of(me.dp * TOK, TOK), TOK)

    @pl.loop(0, LANES // 256)
    def _(i):
        at = pl.ds(pl.multiple_of(i * 256, 256), 256)
        acts = dot(rows[...], w[:, at]) + enc_bias[:, at]
        opened = jax.nn.sigmoid((acts - thr[:, at]) / ramp_width)
        pre[:, at] = acts
        gate[:, at] = opened
        codes[my_rows, at] = (acts * opened).astype(BF16)

    ring_c.start()
    save_codes = pltpu.make_async_copy(codes.at[my_rows], codes_out, local_sem.at[5])
    save_codes.start()
    mine = codes[my_rows, :]

    @pl.loop(0, 16)
    def _(i):
        at = pl.ds(pl.multiple_of(i * WIDTH, 32), WIDTH)
        part2[at, :] = dot_t(w[at, :], mine).astype(BF16)

    ring_c.tick(0)
    gather_st.finish()
    rebuilt = reduce_to_owner(net, me, part2, mate2, out2, got2)
    error = (rebuilt + bias_col[...] - sae_mine[...].astype(F32)).astype(BF16)
    err_mine[...] = error
    feature_rows(err_f, me.t)[...] = error
    gather = Gather(net, me, err_f)
    gather.start()
    turn_e = net.copy(err_mine, turned_e, turn_to)
    turn_e.start()
    ring_c.tick(1)
    gather.finish()
    turn_e.wait_recv()
    feature_rows(err_t, me.t)[...] = turned_e[...]
    gather_et = Gather(net, me, err_t)
    gather_et.start()
    transpose_into(err_f, rows)

    @pl.loop(0, LANES // 256)
    def _(i):
        at = pl.ds(pl.multiple_of(i * 256, 256), 256)
        opened = gate[:, at]
        slope = opened + pre[:, at] * opened * (1.0 - opened) / ramp_width
        grads[my_rows, at] = (dot(rows[...], w[:, at]) * slope).astype(BF16)

    ring_g = Ring(net, me, grads, TOK, 80, 48, 32)
    ring_g.start()
    ring_c.tick(2)
    ring_g.tick(0)
    gather_et.finish()
    ring_c.tick(3)
    ring_c.tick(4)
    ring_c.crossed()
    wg[...] = jnp.zeros_like(wg)

    def accumulate(features, table):
        @pl.loop(0, GROUPS // 4)
        def _(i):
            left = jnp.concatenate(
                [features[pl.ds(pl.multiple_of(((4 * i + j + 1) % 16) * WIDTH, 32), WIDTH), :] for j in range(4)],
                axis=1,
            )

            @pl.loop(0, LANES // 256)
            def _(n):
                at = pl.ds(pl.multiple_of(n * 256, 256), 256)
                wg[:, at] += dot(left, table[pl.ds(pl.multiple_of(i * 4 * TOK, TOK), 4 * TOK), at])

    accumulate(err_t, codes)
    for s in range(1, 5):
        ring_g.tick(s)
    ring_g.crossed()
    accumulate(sae_t, grads)

    grad_scale = 1.0 / math.sqrt(TOKENS)

    def add_rows(i, acc):
        block = grads[pl.ds(pl.multiple_of(i * TOK, TOK), TOK), :].astype(F32)
        return acc + jnp.sum(block, axis=0, keepdims=True)

    bg[...] = grad_scale * lax.fori_loop(0, GROUPS, add_rows, jnp.zeros((1, LANES), F32))
    final[...] = (wg[...] * grad_scale).astype(BF16)
    save_wg = pltpu.make_async_copy(final, wg_out, local_sem.at[6])
    save_wg.start()
    save_bg = pltpu.make_async_copy(bg, bg_out, local_sem.at[7])
    save_bg.start()
    net.close()
    save_codes.wait()
    save_wg.wait()
    save_bg.wait()


def local(
    residual,
    segments,
    row_perm,
    pre_gain,
    post_gain,
    w_query,
    w_key,
    w_value,
    w_out,
    sae_weight,
    enc_bias,
    thresholds,
    dec_bias,
):
    t = lax.axis_index(("tensor", "latent"))

    def column(v):
        mine = lax.dynamic_slice_in_dim(v, t * WIDTH, WIDTH, 0)
        return jnp.broadcast_to(mine[:, None], (WIDTH, TOK))

    vmem = pl.BlockSpec(memory_space=pltpu.VMEM)
    hbm = pl.BlockSpec(memory_space=pl.ANY)
    piece = (WIDTH, TOK)
    whole = (D, TOK)
    wg, bg, codes = pl.pallas_call(
        body,
        out_shape=(
            jax.ShapeDtypeStruct((WIDTH, LANES), BF16),
            jax.ShapeDtypeStruct((1, LANES), F32),
            jax.ShapeDtypeStruct((TOK, LANES), BF16),
        ),
        in_specs=[vmem] * 5 + [hbm] * 5 + [vmem] * 3,
        out_specs=(hbm, hbm, hbm),
        scratch_shapes=[
            pltpu.VMEM((D, 256), BF16),
            pltpu.VMEM((D, 128), BF16),
            pltpu.VMEM((D, 128), BF16),
            pltpu.VMEM((256, D), BF16),
            pltpu.VMEM((D, LANES), BF16),
            pltpu.VMEM(whole, BF16),
            pltpu.VMEM((TOK, D), BF16),
            pltpu.VMEM(whole, BF16),
            pltpu.VMEM((8, *piece), BF16),
            pltpu.VMEM((8, *piece), BF16),
            pltpu.VMEM((8, *piece), BF16),
            pltpu.VMEM(whole, BF16),
            pltpu.VMEM((8, *piece), BF16),
            pltpu.VMEM((8, *piece), BF16),
            pltpu.VMEM((8, *piece), BF16),
            pltpu.VMEM((TOK, TOK), jnp.int32),
            pltpu.VMEM((TOK, TOK), F32),
            pltpu.VMEM((GROUPS, 16, 256), BF16),
            pltpu.VMEM((GROUPS, 16, 256), BF16),
            pltpu.VMEM(whole, BF16),
            pltpu.VMEM(whole, BF16),
            pltpu.VMEM(piece, BF16),
            pltpu.VMEM(piece, BF16),
            pltpu.VMEM(piece, BF16),
            pltpu.VMEM(piece, BF16),
            pltpu.VMEM(whole, BF16),
            pltpu.VMEM(whole, BF16),
            pltpu.VMEM((TOK, LANES), F32),
            pltpu.VMEM((TOK, LANES), F32),
            pltpu.VMEM((TOKENS, LANES), BF16),
            pltpu.VMEM((TOKENS, LANES), BF16),
            pltpu.VMEM((WIDTH, LANES), F32),
            pltpu.VMEM((WIDTH, LANES), BF16),
            pltpu.VMEM((1, LANES), F32),
            pltpu.SemaphoreType.DMA((8,)),
            pltpu.SemaphoreType.DMA((SEMS,)),
            pltpu.SemaphoreType.DMA((SEMS,)),
        ],
        compiler_params=pltpu.CompilerParams(
            collective_id=0, has_side_effects=True, vmem_limit_bytes=60 * 1024 * 1024
        ),
    )(
        residual.T,
        segments,
        row_perm.reshape(1, TOK),
        pre_gain.reshape(1, D),
        column(post_gain),
        w_query,
        w_key,
        w_value,
        w_out,
        sae_weight,
        enc_bias.reshape(1, LANES),
        thresholds.reshape(1, LANES),
        column(dec_bias),
    )
    return wg, bg.reshape(LANES), codes


def solution(mesh):
    features = ("tensor", "latent")
    return jax.shard_map(
        local,
        mesh=mesh,
        in_specs=(
            P("dp", features),
            P("dp", None),
            P("dp"),
            P(),
            P(),
            P(None, features),
            P(None, features),
            P(None, features),
            P(features, None),
            P("dp", features),
            P(features),
            P(features),
            P(),
        ),
        out_specs=(P("dp", features), P(features), P("dp", features)),
        check_vma=False,
    )
```

```python
import math

import jax
import jax.numpy as jnp
from jax import lax
from jax.experimental import pallas as pl
from jax.experimental.pallas import tpu as pltpu
from jax.sharding import PartitionSpec as P

D = 4608
HEADS = 32
HEAD = 128
LANES = 1024
TOK = 128
GROUPS = 16
TOKENS = TOK * GROUPS
BLOCK = 8
WIDTH = D // 16
HALF = D // 2
PAIR = 2 * TOK
SEMS = 300

epsilon = 1e-06
softcap = 50.0
ramp_width = 0.05
rotary_base = 10000.0

MESH = pl.DeviceIdType.MESH
F32 = jnp.float32
BF16 = jnp.bfloat16
ROW_BY_ROW = (((1,), (1,)), ((), ()))


def dot(a, b):
    return jnp.dot(a, b, preferred_element_type=F32)


def dot_t(a, b):
    return lax.dot_general(a, b, ROW_BY_ROW, preferred_element_type=F32)


class Place:
    def __init__(self):
        self.dp = lax.axis_index("dp")
        self.ten = lax.axis_index("tensor")
        self.lat = lax.axis_index("latent")
        self.xl, self.z = self.dp // 8, self.dp % 8
        self.xh, self.core = self.ten // 2, self.ten % 2
        self.t = self.ten * 4 + self.lat
        self.eighth = self.core * 4 + self.lat
        self.half = (self.xl + self.xh) % 2
        self.group = (self.xl + self.xh + 1) % 2

    def at(self, dp=None, ten=None, lat=None):
        return {
            "dp": self.dp if dp is None else dp,
            "tensor": self.ten if ten is None else ten,
            "latent": self.lat if lat is None else lat,
        }

    def at_x(self):
        return self.at(dp=(1 - self.xl) * 8 + self.z)

    def chip(self, k, sign=1):
        return (self.xh + k // 4) % 2, (self.lat + sign * (k % 4) + 4) % 4

    def by_device(self, k, core, sign=1):
        xh, y = self.chip(k, sign)
        return (xh * 2 + core) * 4 + y

    def by_half(self, k, core, sign=1):
        xh, y = self.chip(k, sign)
        return (((self.xl + xh) % 2) * 2 + core) * 4 + y

    def by_group(self, k, core, sign=1):
        xh, y = self.chip(k, sign)
        return (((self.xl + xh + 1) % 2) * 2 + core) * 4 + y

    def peer(self, k, core=None):
        xh, y = self.chip(k)
        return self.at(ten=xh * 2 + (self.core if core is None else core), lat=y)

    def sibling(self):
        return self.at(ten=self.xh * 2 + 1 - self.core)


class Net:
    def __init__(self, send, recv):
        self.send, self.recv, self.used, self.open = send, recv, 0, []

    def copy(self, src, dst, device):
        i = self.used
        self.used += 1
        assert i < SEMS
        c = pltpu.make_async_remote_copy(
            src_ref=src,
            dst_ref=dst,
            send_sem=self.send.at[i],
            recv_sem=self.recv.at[i],
            device_id=device,
            device_id_type=MESH,
        )
        self.open.append(c)
        return c

    def close(self):
        for c in self.open:
            c.wait_send()
        self.open = []


FAR_FIRST = (6, 5, 7, 4, 2, 1, 3)
NEAR_FIRST = (1, 3, 2, 4, 5, 7, 6)


def piece_rows(ref, index):
    return ref.at[pl.ds(pl.multiple_of(index * WIDTH, 32), WIDTH)]


class Gather:
    def __init__(self, net, me, buf, piece):
        self.net, self.me, self.buf, self.piece = net, me, buf, piece

    def send(self, k, device):
        ref = piece_rows(self.buf, self.piece(k, self.me.core, -1))
        c = self.net.copy(ref, ref, device)
        c.start()
        return c

    def start(self):
        me = self.me
        self.first = {k: self.send(0, me.peer(k)) for k in (4, 2, 1, 3)}
        self.near = {0: self.send(0, me.sibling())}

    def finish(self):
        me = self.me
        self.first[4].wait_recv()
        second = {k: self.send(4, me.peer(k)) for k in (2, 1, 3)}
        self.near[4] = self.send(4, me.sibling())
        for k in (1, 3, 2):
            self.first[k].wait_recv()
            self.near[k] = self.send(k, me.sibling())
        for k in (1, 3, 2):
            second[k].wait_recv()
            self.near[4 + k] = self.send(4 + k, me.sibling())
        for c in self.near.values():
            c.wait_recv()


def reduce_to_owner(net, me, piece, part, mate, out, got):
    order = (*FAR_FIRST, 0)
    pair = {}
    for k in order:
        pair[k] = net.copy(piece_rows(part, piece(k, 1 - me.core)), mate.at[k], me.sibling())
        pair[k].start()
    away = {}
    for k in order:
        pair[k].wait_recv()
        both = piece_rows(part, piece(k, me.core))[...].astype(F32) + mate[k].astype(F32)
        if k == 0:
            total = both
        else:
            out[k] = both.astype(BF16)
            away[k] = net.copy(out.at[k], got.at[k], me.peer(k))
            away[k].start()
    for k in NEAR_FIRST:
        away[k].wait_recv()
        total = total + got[k].astype(F32)
    return total


class Ring:
    def __init__(self, net, me, buf, size, width):
        self.net, self.me, self.buf, self.size, self.width = net, me, buf, size, width
        self.moves = {}

    def move(self, chunk, sign, step):
        me = self.me
        lo, count = 0, self.size
        if step == 4:
            count = self.size // 2
            lo = 0 if sign > 0 else count
        block = (me.z - sign * (step - 1) + 8) % 8
        ref = self.buf.at[
            pl.ds(pl.multiple_of(block * self.size + lo, 16), count),
            pl.ds(chunk * self.width, self.width),
        ]
        c = self.net.copy(ref, ref, me.at(dp=me.xl * 8 + (me.z + sign + 8) % 8))
        c.start()
        self.moves[chunk, sign, step] = c

    def start(self, chunk):
        for sign in (1, -1):
            self.move(chunk, sign, 1)

    def tick(self, chunk, step):
        for sign in (1, -1):
            self.moves[chunk, sign, step].wait_recv()
            if step < 4:
                self.move(chunk, sign, step + 1)


def transpose_into(src, dst, count):
    @pl.loop(0, count)
    def _(i):
        at = pl.multiple_of(i * TOK, TOK)
        dst[:, pl.ds(at, TOK)] = src[pl.ds(at, TOK), :].T


def transpose_pair(src, dst):
    @pl.loop(0, HALF // TOK)
    def _(i):
        at = pl.multiple_of(i * TOK, TOK)
        dst[:TOK, pl.ds(at, TOK)] = src[pl.ds(at, TOK), :].T
        dst[TOK:, pl.ds(at, TOK)] = src[pl.ds(HALF + at, TOK), :].T


def body(
    res,
    seg,
    perm,
    pre_gain,
    gain_col,
    wq_hbm,
    wk_hbm,
    wv_hbm,
    wo_hbm,
    w_hbm,
    enc_bias,
    thr,
    bias_col,
    wg_out,
    bg_out,
    codes_out,
    wq,
    wk,
    wv,
    wo,
    w,
    feat,
    rows,
    part,
    mate,
    out,
    got,
    part2,
    mate2,
    out2,
    got2,
    asked,
    squares,
    sent,
    taken,
    sae_f,
    err_f,
    sae_mine,
    err_mine,
    turned_s,
    turned_e,
    sae_t,
    err_t,
    pair_rows,
    acts_here,
    acts_there,
    slope,
    codes2,
    both,
    grad_sent,
    grad_got,
    codes,
    grads,
    left_s,
    left_e,
    wg,
    wg_sent,
    wg_got,
    final,
    bg_here,
    bg_there,
    bg,
    local_sem,
    send_sem,
    recv_sem,
):
    me = Place()
    net = Net(send_sem, recv_sem)

    loads = []
    for i, (src, dst) in enumerate(
        [
            (w_hbm, piece_rows(w, me.z)),
            (wq_hbm, wq),
            (wk_hbm, wk),
            (wv_hbm, wv),
            (wo_hbm, wo),
        ]
    ):
        loads.append(pltpu.make_async_copy(src, dst, local_sem.at[i]))
        loads[-1].start()

    turn = (me.z + 1) % 8
    turn_to = me.at(dp=me.group * 8 + me.eighth, ten=me.xl * 2 + turn // 4, lat=turn % 4)
    turn_from = me.at(dp=me.xh * 8 + (me.eighth + 7) % 8, ten=me.group * 2 + me.z // 4, lat=me.z % 4)

    greeted = [turn_from, me.sibling()]
    for k in range(1, 8):
        for core in range(2):
            greeted.append(me.peer(k, core))

    def dp_peer(j):
        return ((me.xl + j // 8) % 2) * 8 + (me.z + j % 8) % 8

    for j in range(1, 16):
        greeted.append(me.at(dp=dp_peer(j)))
    for j in range(16):
        if j != 8:
            x = (me.group + j // 8) % 2
            z = (me.z + 8 - j % 8) % 8
            greeted.append(me.at(dp=x * 8 + z, ten=((x + me.xl) % 2) * 2 + me.core))
    barrier = pltpu.get_barrier_semaphore()
    for device in greeted:
        pl.semaphore_signal(barrier, inc=1, device_id=device, device_id_type=MESH)

    @pl.when(me.xh == 1)
    def _():
        pl.semaphore_signal(barrier, inc=1, device_id=me.at_x(), device_id_type=MESH)

    pl.semaphore_wait(barrier, len(greeted) + me.xh)

    piece_rows(feat, me.t)[...] = res[...]
    gather = Gather(net, me, feat, me.by_device)
    gather.start()

    def eight_rows(ref, index):
        return ref.at[pl.ds(pl.multiple_of(index * 8, 8), 8)]

    eight_rows(asked, me.dp)[...] = jnp.broadcast_to(perm[...], (8, TOK))
    asks = []
    for j in range(1, 16):
        own = eight_rows(asked, me.dp)
        asks.append(net.copy(own, own, me.at(dp=dp_peer(j))))
        asks[-1].start()

    loads[0].wait()
    ring = Ring(net, me, w, WIDTH, 512)
    ring.start(0)
    ring.start(1)

    lane = lax.broadcasted_iota(jnp.int32, (TOK, TOK), 1)
    row = lax.broadcasted_iota(jnp.int32, (TOK, TOK), 0)
    seg_k = jnp.broadcast_to(seg[...].astype(F32), (TOK, TOK))
    same = seg_k == seg_k.T
    position = jnp.sum(jnp.where(same & (lane < row), 1.0, 0.0), axis=1, keepdims=True)
    allowed = same & (lane <= row)
    step = (lane % 64).astype(F32)
    angle = position * jnp.exp(step * (-2.0 / HEAD * math.log(rotary_base)))
    cosine = jnp.cos(angle)
    sine = jnp.sin(angle)
    sine = jnp.where(lane < 64, -sine, sine)

    for c in asks:
        c.wait_recv()
    place = 8 * me.dp + row % 8
    mine = jnp.where(lane == place, asked[...], 0).astype(F32)
    number = jnp.sum(mine, axis=1, keepdims=True) - (me.dp * TOK).astype(F32)
    pick = jnp.where(number == lane.astype(F32), 1.0, 0.0).astype(BF16)

    gather.finish()
    ring.tick(0, 1)
    transpose_into(feat, rows, D // TOK)

    def add_squares(i, acc):
        x = rows[:, pl.ds(pl.multiple_of(i * TOK, TOK), TOK)].astype(F32)
        return acc + x * x

    acc = lax.fori_loop(0, D // TOK, add_squares, jnp.zeros((TOK, TOK), F32), unroll=4)
    scale = lax.rsqrt(jnp.sum(acc, axis=1, keepdims=True) * (1.0 / D) + epsilon)

    @pl.loop(0, D // TOK, unroll=4)
    def _(i):
        at = pl.ds(pl.multiple_of(i * TOK, TOK), TOK)
        rows[:, at] = (rows[:, at].astype(F32) * scale * pre_gain[:, at]).astype(BF16)

    for c in loads[1:]:
        c.wait()
    normed = rows[...]
    query = dot(normed, wq[...])
    key = dot(normed, wk[...])
    value = dot(normed, wv[...]).astype(BF16)

    def rotate(v):
        return (v * cosine + pltpu.roll(v, 64, 1) * sine).astype(BF16)

    key = rotate(key)
    heads = []
    for h in range(2):
        q = rotate(query[:, h * HEAD : (h + 1) * HEAD])
        scores = dot_t(q, key) * (D / HEADS) ** (-0.5)
        scores = softcap * jnp.tanh(scores / softcap)
        weighted = jnp.where(allowed, jnp.exp(scores), 0.0)
        probs = (weighted / jnp.sum(weighted, axis=1, keepdims=True)).astype(BF16)
        heads.append(dot(probs, value).astype(BF16))
    heads = jnp.concatenate(heads, axis=1)

    ring.tick(1, 1)

    @pl.loop(0, D // 256)
    def _(i):
        at = pl.multiple_of(i * 256, 256)
        part[pl.ds(at, 256), :] = dot(heads, wo[:, pl.ds(at, 256)]).astype(BF16).T

    attn = reduce_to_owner(net, me, me.by_half, part, mate, out, got)

    total = jnp.sum(attn * attn, axis=0, keepdims=True)
    own = eight_rows(squares, me.t)
    own[...] = jnp.broadcast_to(total, (8, TOK))
    sums = []
    for k in range(8):
        for core in range(2):
            if k or core:
                device = me.peer(k, (me.core + core) % 2)
                sums.append(net.copy(own, own, device))
                sums[-1].start()
    ring.tick(0, 2)
    for c in sums:
        c.wait_recv()
    ring.tick(1, 2)
    total = jnp.sum(squares[...], axis=0, keepdims=True) * (0.125 / D)
    stream = piece_rows(feat, me.half * 8 + me.eighth)[...].astype(F32)
    hidden = stream + attn * lax.rsqrt(total + epsilon) * gain_col[...]
    hidden = hidden.astype(BF16)

    low = dot_t(pick, hidden[:256])
    high = dot_t(pick, hidden[32:])
    for g in range(GROUPS):
        block = jnp.concatenate([low[8 * g : 8 * g + 8], high[8 * g : 8 * g + 8]], axis=0)
        sent[g] = block.astype(BF16)
    moves = []
    to = dp_peer(8)
    other = net.copy(sent.at[to], taken.at[me.dp], me.at_x())
    net.open.pop()

    @pl.when(me.xh == 1)
    def _():
        other.start()

    @pl.when(me.xh == 0)
    def _():
        taken[me.dp] = sent[to]

    for j in (15, 14, 13, 12, 11, 10, 9, 4, 3, 5, 2, 6, 1, 7, 0):
        to = dp_peer(j)
        x, z = to // 8, to % 8
        ten = ((x + me.half + 1) % 2) * 2 + me.core
        moves.append(net.copy(sent.at[to], taken.at[me.dp], me.at(dp=me.half * 8 + z, ten=ten)))
        moves[-1].start()

    @pl.when(me.xh == 1)
    def _():
        other.wait()

    for c in moves:
        c.wait_recv()
    low, high = [], []
    for g in range(GROUPS):
        block = taken[g].astype(F32)
        low.append(block[:8])
        high.append(block[8:, 128:])
    low = jnp.concatenate(low, axis=0)
    high = jnp.concatenate(high, axis=0)
    sae_mine[...] = jnp.concatenate([low.T, high.T[96:]], axis=0).astype(BF16)
    piece_rows(sae_f, me.group * 8 + me.eighth)[...] = sae_mine[...]
    gather = Gather(net, me, sae_f, me.by_group)
    gather.start()
    ring.tick(0, 3)
    ring.tick(1, 3)
    gather.finish()
    turn_s = net.copy(sae_mine, turned_s, turn_to)
    turn_s.start()
    transpose_pair(sae_f, pair_rows)
    ring.tick(0, 4)
    ring.tick(1, 4)

    swaps = []
    for n in range(4):
        at = slice(256 * n, 256 * n + 256)
        acts_here[n] = dot(pair_rows[...], w[:, at]).astype(BF16)
        swaps.append(net.copy(acts_here.at[n], acts_there.at[n], me.at_x()))
        swaps[-1].start()
    turn_s.wait_recv()
    piece_rows(sae_t, me.t)[...] = turned_s[...]
    gather_st = Gather(net, me, sae_t, me.by_device)
    for n in range(4):
        at = slice(256 * n, 256 * n + 256)
        swaps[n].wait_recv()
        acts = acts_here[n].astype(F32) + acts_there[n].astype(F32) + enc_bias[:, at]
        opened = jax.nn.sigmoid((acts - thr[:, at]) / ramp_width)
        slope[:, at] = opened + acts * opened * (1.0 - opened) / ramp_width
        codes2[:, at] = (acts * opened).astype(BF16)
    my_rows = pl.ds(pl.multiple_of(me.xl * TOK, TOK), TOK)
    my_block = pl.ds(pl.multiple_of(me.z * TOK, TOK), TOK)
    codes[my_block, :] = codes2[my_rows, :]
    ring_c = Ring(net, me, codes, TOK, 512)
    ring_c.start(0)
    ring_c.start(1)
    save_codes = pltpu.make_async_copy(codes.at[my_block], codes_out, local_sem.at[5])
    save_codes.start()
    mine = codes2[...]

    @pl.loop(0, 8)
    def _(i):
        at = pl.ds(pl.multiple_of(i * WIDTH, 32), WIDTH)
        rebuilt = dot_t(w[at, :], mine).astype(BF16)
        part2[at, :] = rebuilt[:, :TOK]
        part2[pl.ds(pl.multiple_of(HALF + i * WIDTH, 32), WIDTH), :] = rebuilt[:, TOK:]

    rebuilt = reduce_to_owner(net, me, me.by_group, part2, mate2, out2, got2)
    error = (rebuilt + bias_col[...] - sae_mine[...].astype(F32)).astype(BF16)
    err_mine[...] = error
    piece_rows(err_f, me.group * 8 + me.eighth)[...] = error
    gather = Gather(net, me, err_f, me.by_group)
    gather.start()
    ring_c.tick(0, 1)
    ring_c.tick(1, 1)
    gather.finish()
    turn_e = net.copy(err_mine, turned_e, turn_to)
    turn_e.start()
    gather_st.start()
    transpose_pair(err_f, pair_rows)
    swaps = []
    mates_rows = pl.ds(pl.multiple_of((1 - me.xl) * TOK, TOK), TOK)
    for n in range(4):
        both[n] = dot(pair_rows[...], w[:, 256 * n : 256 * n + 256])
        grad_sent[n] = both[n, mates_rows, :].astype(BF16)
        swaps.append(net.copy(grad_sent.at[n], grad_got.at[n], me.at_x()))
        swaps[-1].start()
        if n == 0:
            ring_c.tick(0, 2)
        if n == 1:
            ring_c.tick(1, 2)
    ring_g = Ring(net, me, grads, TOK, 256)

    def finish_grads(n):
        at = slice(256 * n, 256 * n + 256)
        swaps[n].wait_recv()
        product = both[n, my_rows, :] + grad_got[n].astype(F32)
        grads[my_block, at] = (product * slope[my_rows, at]).astype(BF16)

    for n in range(4):
        finish_grads(n)
        if n < 2:
            ring_g.start(n)
    ring_c.tick(0, 3)
    ring_c.tick(1, 3)
    ring_g.tick(0, 1)
    turn_e.wait_recv()
    piece_rows(err_t, me.t)[...] = turned_e[...]
    gather_et = Gather(net, me, err_t, me.by_device)
    gather_et.start()
    gather_st.finish()
    ring_g.tick(1, 1)
    ring_c.tick(0, 4)
    ring_c.tick(1, 4)
    gather_et.finish()
    ring_g.tick(0, 2)

    def side_by_side(src, dst):
        for f in range(2):
            for z in range(8):
                at = (f * 8 + (z + 1) % 8) * WIDTH
                dst[f, :, z * TOK : (z + 1) * TOK] = src[at : at + WIDTH, :]

    side_by_side(sae_t, left_s)
    side_by_side(err_t, left_e)
    for f in range(2):
        for n in range(4):
            at = slice(256 * n, 256 * n + 256)
            wg[f, :, at] = dot(left_e[f], codes[:, at])

    grad_scale = 1.0 / math.sqrt(TOKENS)
    ones = jnp.ones((8, 8 * TOK), BF16)
    swaps = []

    def finish_columns(n):
        at = slice(256 * n, 256 * n + 256)
        mates = 1 - me.xl
        table = grads[:, at]
        theirs = wg[mates, :, at] + dot(left_s[mates], table)
        wg_sent[n] = (theirs * grad_scale).astype(BF16)
        swaps.append(net.copy(wg_sent.at[n], wg_got.at[n], me.at_x()))
        swaps[-1].start()
        wg[me.xl, :, at] += dot(left_s[me.xl], table)
        bg_here[:, at] = dot(ones, table)

    def save_columns(n):
        at = slice(256 * n, 256 * n + 256)
        swaps[n].wait_recv()
        final[:, at] = (wg[me.xl, :, at] * grad_scale + wg_got[n].astype(F32)).astype(BF16)

    ring_g.tick(1, 2)
    ring_g.tick(0, 3)
    ring_g.start(2)
    ring_g.tick(1, 3)
    ring_g.start(3)
    ring_g.tick(0, 4)
    ring_g.tick(2, 1)
    finish_columns(0)
    ring_g.tick(1, 4)
    ring_g.tick(3, 1)
    finish_columns(1)
    ring_g.tick(2, 2)
    ring_g.tick(3, 2)
    save_columns(0)
    ring_g.tick(2, 3)
    ring_g.tick(3, 3)
    ring_g.tick(2, 4)
    finish_columns(2)
    ring_g.tick(3, 4)
    finish_columns(3)
    bias_swap = net.copy(bg_here, bg_there, me.at_x())
    bias_swap.start()
    save_columns(1)
    save_columns(2)
    save_columns(3)
    save_wg = pltpu.make_async_copy(final, wg_out, local_sem.at[6])
    save_wg.start()
    bias_swap.wait_recv()
    bg[...] = grad_scale * (bg_here[0:1, :] + bg_there[0:1, :])
    save_bg = pltpu.make_async_copy(bg, bg_out, local_sem.at[7])
    save_bg.start()
    net.close()
    save_codes.wait()
    save_wg.wait()
    save_bg.wait()


def local(
    residual,
    segments,
    row_perm,
    pre_gain,
    post_gain,
    w_query,
    w_key,
    w_value,
    w_out,
    sae_weight,
    enc_bias,
    thresholds,
    dec_bias,
):
    x, core_y = lax.axis_index("dp") // 8, lax.axis_index(("tensor", "latent"))
    half = (x + core_y // 8) % 2

    def column(v, half):
        mine = lax.dynamic_slice_in_dim(v, (half * 8 + core_y % 8) * WIDTH, WIDTH, 0)
        return jnp.broadcast_to(mine[:, None], (WIDTH, TOK))

    vmem = pl.BlockSpec(memory_space=pltpu.VMEM)
    hbm = pl.BlockSpec(memory_space=pl.ANY)
    piece = (WIDTH, TOK)
    whole = (D, TOK)
    wg, bg, codes = pl.pallas_call(
        body,
        out_shape=(
            jax.ShapeDtypeStruct((WIDTH, LANES), BF16),
            jax.ShapeDtypeStruct((1, LANES), F32),
            jax.ShapeDtypeStruct((TOK, LANES), BF16),
        ),
        in_specs=[vmem] * 5 + [hbm] * 5 + [vmem] * 3,
        out_specs=(hbm, hbm, hbm),
        scratch_shapes=[
            pltpu.VMEM((D, 256), BF16),
            pltpu.VMEM((D, 128), BF16),
            pltpu.VMEM((D, 128), BF16),
            pltpu.VMEM((256, D), BF16),
            pltpu.VMEM((HALF, LANES), BF16),
            pltpu.VMEM(whole, BF16),
            pltpu.VMEM((TOK, D), BF16),
            pltpu.VMEM(whole, BF16),
            pltpu.VMEM((8, *piece), BF16),
            pltpu.VMEM((8, *piece), BF16),
            pltpu.VMEM((8, *piece), BF16),
            pltpu.VMEM(whole, BF16),
            pltpu.VMEM((8, *piece), BF16),
            pltpu.VMEM((8, *piece), BF16),
            pltpu.VMEM((8, *piece), BF16),
            pltpu.VMEM((TOK, TOK), jnp.int32),
            pltpu.VMEM((TOK, TOK), F32),
            pltpu.VMEM((GROUPS, 16, 256), BF16),
            pltpu.VMEM((GROUPS, 16, 256), BF16),
            pltpu.VMEM(whole, BF16),
            pltpu.VMEM(whole, BF16),
            pltpu.VMEM(piece, BF16),
            pltpu.VMEM(piece, BF16),
            pltpu.VMEM(piece, BF16),
            pltpu.VMEM(piece, BF16),
            pltpu.VMEM(whole, BF16),
            pltpu.VMEM(whole, BF16),
            pltpu.VMEM((PAIR, HALF), BF16),
            pltpu.VMEM((4, PAIR, 256), BF16),
            pltpu.VMEM((4, PAIR, 256), BF16),
            pltpu.VMEM((PAIR, LANES), F32),
            pltpu.VMEM((PAIR, LANES), BF16),
            pltpu.VMEM((4, PAIR, 256), F32),
            pltpu.VMEM((4, TOK, 256), BF16),
            pltpu.VMEM((4, TOK, 256), BF16),
            pltpu.VMEM((8 * TOK, LANES), BF16),
            pltpu.VMEM((8 * TOK, LANES), BF16),
            pltpu.VMEM((2, WIDTH, 8 * TOK), BF16),
            pltpu.VMEM((2, WIDTH, 8 * TOK), BF16),
            pltpu.VMEM((2, WIDTH, LANES), F32),
            pltpu.VMEM((4, WIDTH, 256), BF16),
            pltpu.VMEM((4, WIDTH, 256), BF16),
            pltpu.VMEM((WIDTH, LANES), BF16),
            pltpu.VMEM((8, LANES), F32),
            pltpu.VMEM((8, LANES), F32),
            pltpu.VMEM((1, LANES), F32),
            pltpu.SemaphoreType.DMA((8,)),
            pltpu.SemaphoreType.DMA((SEMS,)),
            pltpu.SemaphoreType.DMA((SEMS,)),
        ],
        compiler_params=pltpu.CompilerParams(
            collective_id=0, has_side_effects=True, vmem_limit_bytes=60 * 1024 * 1024
        ),
    )(
        residual.T,
        segments,
        row_perm.reshape(1, TOK),
        pre_gain.reshape(1, D),
        column(post_gain, half),
        w_query,
        w_key,
        w_value,
        w_out,
        sae_weight,
        enc_bias.reshape(1, LANES),
        thresholds.reshape(1, LANES),
        column(dec_bias, x),
    )
    return wg, bg.reshape(LANES), codes


def solution(mesh):
    features = ("tensor", "latent")
    return jax.shard_map(
        local,
        mesh=mesh,
        in_specs=(
            P("dp", features),
            P("dp", None),
            P("dp"),
            P(),
            P(),
            P(None, features),
            P(None, features),
            P(None, features),
            P(features, None),
            P("dp", features),
            P(features),
            P(features),
            P(),
        ),
        out_specs=(P("dp", features), P(features), P("dp", features)),
        check_vma=False,
    )
```

```python
import math

import jax
import jax.numpy as jnp
from jax import lax
from jax.experimental import pallas as pl
from jax.experimental.pallas import tpu as pltpu
from jax.sharding import PartitionSpec as P

D = 4608
HEADS = 32
HEAD = 128
LANES = 1024
TOK = 128
GROUPS = 16
TOKENS = TOK * GROUPS
BLOCK = 8
WIDTH = D // 16
HALF = D // 2
PAIR = 2 * TOK
SEMS = 300

epsilon = 1e-06
softcap = 50.0
ramp_width = 0.05
rotary_base = 10000.0

MESH = pl.DeviceIdType.MESH
F32 = jnp.float32
BF16 = jnp.bfloat16
ROW_BY_ROW = (((1,), (1,)), ((), ()))


def dot(a, b):
    return jnp.dot(a, b, preferred_element_type=F32)


def dot_t(a, b):
    return lax.dot_general(a, b, ROW_BY_ROW, preferred_element_type=F32)


class Place:
    def __init__(self):
        self.dp = lax.axis_index("dp")
        self.ten = lax.axis_index("tensor")
        self.lat = lax.axis_index("latent")
        self.xl, self.z = self.dp // 8, self.dp % 8
        self.xh, self.core = self.ten // 2, self.ten % 2
        self.t = self.ten * 4 + self.lat
        self.eighth = self.core * 4 + self.lat
        self.half = (self.xl + self.xh) % 2
        self.group = (self.xl + self.xh + 1) % 2

    def at(self, dp=None, ten=None, lat=None):
        return {
            "dp": self.dp if dp is None else dp,
            "tensor": self.ten if ten is None else ten,
            "latent": self.lat if lat is None else lat,
        }

    def at_x(self):
        return self.at(dp=(1 - self.xl) * 8 + self.z)

    def chip(self, k, sign=1):
        return (self.xh + k // 4) % 2, (self.lat + sign * (k % 4) + 4) % 4

    def by_device(self, k, core, sign=1):
        xh, y = self.chip(k, sign)
        return (xh * 2 + core) * 4 + y

    def by_half(self, k, core, sign=1):
        xh, y = self.chip(k, sign)
        return (((self.xl + xh) % 2) * 2 + core) * 4 + y

    def by_group(self, k, core, sign=1):
        xh, y = self.chip(k, sign)
        return (((self.xl + xh + 1) % 2) * 2 + core) * 4 + y

    def peer(self, k, core=None):
        xh, y = self.chip(k)
        return self.at(ten=xh * 2 + (self.core if core is None else core), lat=y)

    def sibling(self):
        return self.at(ten=self.xh * 2 + 1 - self.core)


class Net:
    def __init__(self, send, recv):
        self.send, self.recv, self.used, self.open = send, recv, 0, []

    def copy(self, src, dst, device):
        i = self.used
        self.used += 1
        assert i < SEMS
        c = pltpu.make_async_remote_copy(
            src_ref=src,
            dst_ref=dst,
            send_sem=self.send.at[i],
            recv_sem=self.recv.at[i],
            device_id=device,
            device_id_type=MESH,
        )
        self.open.append(c)
        return c

    def close(self):
        for c in self.open:
            c.wait_send()
        self.open = []


FAR_FIRST = (6, 5, 7, 4, 2, 1, 3)
NEAR_FIRST = (1, 3, 2, 4, 5, 7, 6)


def piece_rows(ref, index):
    return ref.at[pl.ds(pl.multiple_of(index * WIDTH, 32), WIDTH)]


class Gather:
    def __init__(self, net, me, buf, piece):
        self.net, self.me, self.buf, self.piece = net, me, buf, piece

    def send(self, k, device):
        ref = piece_rows(self.buf, self.piece(k, self.me.core, -1))
        c = self.net.copy(ref, ref, device)
        c.start()
        return c

    def start(self):
        me = self.me
        self.first = {k: self.send(0, me.peer(k)) for k in (4, 2, 1, 3)}
        self.near = {0: self.send(0, me.sibling())}

    def finish(self):
        me = self.me
        self.first[4].wait_recv()
        second = {k: self.send(4, me.peer(k)) for k in (2, 1, 3)}
        self.near[4] = self.send(4, me.sibling())
        for k in (1, 3, 2):
            self.first[k].wait_recv()
            self.near[k] = self.send(k, me.sibling())
        for k in (1, 3, 2):
            second[k].wait_recv()
            self.near[4 + k] = self.send(4 + k, me.sibling())
        for c in self.near.values():
            c.wait_recv()


def reduce_to_owner(net, me, piece, part, mate, out, got):
    order = (*FAR_FIRST, 0)
    pair = {}
    for k in order:
        pair[k] = net.copy(piece_rows(part, piece(k, 1 - me.core)), mate.at[k], me.sibling())
        pair[k].start()
    away = {}
    for k in order:
        pair[k].wait_recv()
        both = piece_rows(part, piece(k, me.core))[...].astype(F32) + mate[k].astype(F32)
        if k == 0:
            total = both
        else:
            out[k] = both.astype(BF16)
            away[k] = net.copy(out.at[k], got.at[k], me.peer(k))
            away[k].start()
    for k in NEAR_FIRST:
        away[k].wait_recv()
        total = total + got[k].astype(F32)
    return total


class Ring:
    def __init__(self, net, me, buf, size, width):
        self.net, self.me, self.buf, self.size, self.width = net, me, buf, size, width
        self.moves = {}

    def move(self, chunk, sign, step):
        me = self.me
        lo, count = 0, self.size
        if step == 4:
            count = self.size // 2
            lo = 0 if sign > 0 else count
        block = (me.z - sign * (step - 1) + 8) % 8
        ref = self.buf.at[
            pl.ds(pl.multiple_of(block * self.size + lo, 16), count),
            pl.ds(chunk * self.width, self.width),
        ]
        c = self.net.copy(ref, ref, me.at(dp=me.xl * 8 + (me.z + sign + 8) % 8))
        c.start()
        self.moves[chunk, sign, step] = c

    def start(self, chunk):
        for sign in (1, -1):
            self.move(chunk, sign, 1)

    def tick(self, chunk, step):
        for sign in (1, -1):
            self.moves[chunk, sign, step].wait_recv()
            if step < 4:
                self.move(chunk, sign, step + 1)


def spread(vec, piece, col):
    for i in range(3):
        row = vec[pl.ds(piece * 9 // 4 + i, 1), :]
        col[i * TOK : (i + 1) * TOK, :] = jnp.broadcast_to(row, (TOK, TOK)).T
    return pl.ds(pl.multiple_of(piece % 4 * 32, 32), WIDTH)


def transpose_into(src, dst, count):
    @pl.loop(0, count)
    def _(i):
        at = pl.multiple_of(i * TOK, TOK)
        dst[:, pl.ds(at, TOK)] = src[pl.ds(at, TOK), :].T


def transpose_pair(src, dst):
    @pl.loop(0, HALF // TOK)
    def _(i):
        at = pl.multiple_of(i * TOK, TOK)
        dst[:TOK, pl.ds(at, TOK)] = src[pl.ds(at, TOK), :].T
        dst[TOK:, pl.ds(at, TOK)] = src[pl.ds(HALF + at, TOK), :].T


def body(
    res,
    seg,
    perm,
    pre_gain,
    post_gain,
    wq_hbm,
    wk_hbm,
    wv_hbm,
    wo_hbm,
    w_hbm,
    enc_bias,
    thr,
    dec_bias,
    wg_out,
    bg_out,
    codes_out,
    wq,
    wk,
    wv,
    wo,
    w,
    gain_col,
    bias_col,
    feat,
    rows,
    part,
    mate,
    out,
    got,
    part2,
    mate2,
    out2,
    got2,
    asked,
    squares,
    sent,
    taken,
    sae_f,
    err_f,
    sae_mine,
    err_mine,
    turned_s,
    turned_e,
    sae_t,
    err_t,
    pair_rows,
    acts_here,
    acts_there,
    slope,
    codes2,
    both,
    grad_sent,
    grad_got,
    codes,
    grads,
    left_s,
    left_e,
    wg,
    wg_sent,
    wg_got,
    final,
    bg_here,
    bg_there,
    bg,
    local_sem,
    send_sem,
    recv_sem,
):
    me = Place()
    net = Net(send_sem, recv_sem)

    loads = []
    for i, (src, dst) in enumerate(
        [
            (w_hbm, piece_rows(w, me.z)),
            (wq_hbm, wq),
            (wk_hbm, wk),
            (wv_hbm, wv),
            (wo_hbm, wo),
        ]
    ):
        loads.append(pltpu.make_async_copy(src, dst, local_sem.at[i]))
        loads[-1].start()

    turn = (me.z + 1) % 8
    turn_to = me.at(dp=me.group * 8 + me.eighth, ten=me.xl * 2 + turn // 4, lat=turn % 4)
    turn_from = me.at(dp=me.xh * 8 + (me.eighth + 7) % 8, ten=me.group * 2 + me.z // 4, lat=me.z % 4)

    greeted = [turn_from, me.sibling()]
    for k in range(1, 8):
        for core in range(2):
            greeted.append(me.peer(k, core))

    def dp_peer(j):
        return ((me.xl + j // 8) % 2) * 8 + (me.z + j % 8) % 8

    for j in range(1, 16):
        greeted.append(me.at(dp=dp_peer(j)))
    for j in range(16):
        if j != 8:
            x = (me.group + j // 8) % 2
            z = (me.z + 8 - j % 8) % 8
            greeted.append(me.at(dp=x * 8 + z, ten=((x + me.xl) % 2) * 2 + me.core))
    barrier = pltpu.get_barrier_semaphore()
    for device in greeted:
        pl.semaphore_signal(barrier, inc=1, device_id=device, device_id_type=MESH)

    @pl.when(me.xh == 1)
    def _():
        pl.semaphore_signal(barrier, inc=1, device_id=me.at_x(), device_id_type=MESH)

    pl.semaphore_wait(barrier, len(greeted) + me.xh)

    piece_rows(feat, me.t)[...] = res[...]
    gather = Gather(net, me, feat, me.by_device)
    gather.start()

    def eight_rows(ref, index):
        return ref.at[pl.ds(pl.multiple_of(index * 8, 8), 8)]

    eight_rows(asked, me.dp)[...] = jnp.broadcast_to(perm[...], (8, TOK))
    asks = []
    for j in range(1, 16):
        own = eight_rows(asked, me.dp)
        asks.append(net.copy(own, own, me.at(dp=dp_peer(j))))
        asks[-1].start()

    loads[0].wait()
    ring = Ring(net, me, w, WIDTH, 512)
    ring.start(0)
    ring.start(1)

    lane = lax.broadcasted_iota(jnp.int32, (TOK, TOK), 1)
    row = lax.broadcasted_iota(jnp.int32, (TOK, TOK), 0)
    seg_k = jnp.broadcast_to(seg[...].astype(F32), (TOK, TOK))
    same = seg_k == seg_k.T
    position = jnp.sum(jnp.where(same & (lane < row), 1.0, 0.0), axis=1, keepdims=True)
    allowed = same & (lane <= row)
    step = (lane % 64).astype(F32)
    angle = position * jnp.exp(step * (-2.0 / HEAD * math.log(rotary_base)))
    cosine = jnp.cos(angle)
    sine = jnp.sin(angle)
    sine = jnp.where(lane < 64, -sine, sine)

    gain_at = spread(post_gain, me.half * 8 + me.eighth, gain_col)
    bias_at = spread(dec_bias, me.xl * 8 + me.eighth, bias_col)

    for c in asks:
        c.wait_recv()
    place = 8 * me.dp + row % 8
    mine = jnp.where(lane == place, asked[...], 0).astype(F32)
    number = jnp.sum(mine, axis=1, keepdims=True) - (me.dp * TOK).astype(F32)
    pick = jnp.where(number == lane.astype(F32), 1.0, 0.0).astype(BF16)

    gather.finish()
    ring.tick(0, 1)
    transpose_into(feat, rows, D // TOK)

    def add_squares(i, acc):
        x = rows[:, pl.ds(pl.multiple_of(i * TOK, TOK), TOK)].astype(F32)
        return acc + x * x

    acc = lax.fori_loop(0, D // TOK, add_squares, jnp.zeros((TOK, TOK), F32), unroll=4)
    scale = lax.rsqrt(jnp.sum(acc, axis=1, keepdims=True) * (1.0 / D) + epsilon)

    @pl.loop(0, D // TOK, unroll=4)
    def _(i):
        at = pl.ds(pl.multiple_of(i * TOK, TOK), TOK)
        rows[:, at] = (rows[:, at].astype(F32) * scale * pre_gain[pl.ds(i, 1), :]).astype(BF16)

    for c in loads[1:]:
        c.wait()
    normed = rows[...]
    query = dot(normed, wq[...])
    key = dot(normed, wk[...])
    value = dot(normed, wv[...]).astype(BF16)

    def rotate(v):
        return (v * cosine + pltpu.roll(v, 64, 1) * sine).astype(BF16)

    key = rotate(key)
    heads = []
    for h in range(2):
        q = rotate(query[:, h * HEAD : (h + 1) * HEAD])
        scores = dot_t(q, key) * (D / HEADS) ** (-0.5)
        scores = softcap * jnp.tanh(scores / softcap)
        weighted = jnp.where(allowed, jnp.exp(scores), 0.0)
        probs = (weighted / jnp.sum(weighted, axis=1, keepdims=True)).astype(BF16)
        heads.append(dot(probs, value).astype(BF16))
    heads = jnp.concatenate(heads, axis=1)

    ring.tick(1, 1)

    @pl.loop(0, D // 256)
    def _(i):
        at = pl.multiple_of(i * 256, 256)
        part[pl.ds(at, 256), :] = dot(heads, wo[:, pl.ds(at, 256)]).astype(BF16).T

    attn = reduce_to_owner(net, me, me.by_half, part, mate, out, got)

    total = jnp.sum(attn * attn, axis=0, keepdims=True)
    own = eight_rows(squares, me.t)
    own[...] = jnp.broadcast_to(total, (8, TOK))
    sums = []
    for k in range(8):
        for core in range(2):
            if k or core:
                device = me.peer(k, (me.core + core) % 2)
                sums.append(net.copy(own, own, device))
                sums[-1].start()
    ring.tick(0, 2)
    for c in sums:
        c.wait_recv()
    ring.tick(1, 2)
    total = jnp.sum(squares[...], axis=0, keepdims=True) * (0.125 / D)
    stream = piece_rows(feat, me.half * 8 + me.eighth)[...].astype(F32)
    hidden = stream + attn * lax.rsqrt(total + epsilon) * gain_col[gain_at, :]
    hidden = hidden.astype(BF16)

    low = dot_t(pick, hidden[:256])
    high = dot_t(pick, hidden[32:])
    for g in range(GROUPS):
        block = jnp.concatenate([low[8 * g : 8 * g + 8], high[8 * g : 8 * g + 8]], axis=0)
        sent[g] = block.astype(BF16)
    moves = []
    to = dp_peer(8)
    other = net.copy(sent.at[to], taken.at[me.dp], me.at_x())
    net.open.pop()

    @pl.when(me.xh == 1)
    def _():
        other.start()

    @pl.when(me.xh == 0)
    def _():
        taken[me.dp] = sent[to]

    for j in (15, 14, 13, 12, 11, 10, 9, 4, 3, 5, 2, 6, 1, 7, 0):
        to = dp_peer(j)
        x, z = to // 8, to % 8
        ten = ((x + me.half + 1) % 2) * 2 + me.core
        moves.append(net.copy(sent.at[to], taken.at[me.dp], me.at(dp=me.half * 8 + z, ten=ten)))
        moves[-1].start()

    @pl.when(me.xh == 1)
    def _():
        other.wait()

    for c in moves:
        c.wait_recv()
    low, high = [], []
    for g in range(GROUPS):
        block = taken[g].astype(F32)
        low.append(block[:8])
        high.append(block[8:, 128:])
    low = jnp.concatenate(low, axis=0)
    high = jnp.concatenate(high, axis=0)
    sae_mine[...] = jnp.concatenate([low.T, high.T[96:]], axis=0).astype(BF16)
    piece_rows(sae_f, me.group * 8 + me.eighth)[...] = sae_mine[...]
    gather = Gather(net, me, sae_f, me.by_group)
    gather.start()
    ring.tick(0, 3)
    ring.tick(1, 3)
    gather.finish()
    turn_s = net.copy(sae_mine, turned_s, turn_to)
    turn_s.start()
    transpose_pair(sae_f, pair_rows)
    ring.tick(0, 4)
    ring.tick(1, 4)

    swaps = []
    for n in range(4):
        at = slice(256 * n, 256 * n + 256)
        acts_here[n] = dot(pair_rows[...], w[:, at]).astype(BF16)
        swaps.append(net.copy(acts_here.at[n], acts_there.at[n], me.at_x()))
        swaps[-1].start()
    turn_s.wait_recv()
    piece_rows(sae_t, me.t)[...] = turned_s[...]
    gather_st = Gather(net, me, sae_t, me.by_device)
    gather_st.start()
    for n in range(4):
        at = slice(256 * n, 256 * n + 256)
        swaps[n].wait_recv()
        acts = acts_here[n].astype(F32) + acts_there[n].astype(F32) + enc_bias[:, at]
        opened = jax.nn.sigmoid((acts - thr[:, at]) / ramp_width)
        slope[:, at] = opened + acts * opened * (1.0 - opened) / ramp_width
        codes2[:, at] = (acts * opened).astype(BF16)
    my_rows = pl.ds(pl.multiple_of(me.xl * TOK, TOK), TOK)
    my_block = pl.ds(pl.multiple_of(me.z * TOK, TOK), TOK)
    codes[my_block, :] = codes2[my_rows, :]
    ring_c = Ring(net, me, codes, TOK, 512)
    ring_c.start(0)
    ring_c.start(1)
    save_codes = pltpu.make_async_copy(codes.at[my_block], codes_out, local_sem.at[5])
    save_codes.start()
    mine = codes2[...]

    @pl.loop(0, 8)
    def _(i):
        at = pl.ds(pl.multiple_of(i * WIDTH, 32), WIDTH)
        rebuilt = dot_t(w[at, :], mine).astype(BF16)
        part2[at, :] = rebuilt[:, :TOK]
        part2[pl.ds(pl.multiple_of(HALF + i * WIDTH, 32), WIDTH), :] = rebuilt[:, TOK:]

    gather_st.finish()
    ring_c.tick(0, 1)
    ring_c.tick(1, 1)
    rebuilt = reduce_to_owner(net, me, me.by_group, part2, mate2, out2, got2)
    error = (rebuilt + bias_col[bias_at, :] - sae_mine[...].astype(F32)).astype(BF16)
    err_mine[...] = error
    piece_rows(err_f, me.group * 8 + me.eighth)[...] = error
    gather = Gather(net, me, err_f, me.by_group)
    gather.start()
    turn_e = net.copy(err_mine, turned_e, turn_to)
    turn_e.start()
    ring_c.tick(0, 2)
    ring_c.tick(1, 2)
    gather.finish()
    ring_c.tick(0, 3)
    ring_c.tick(1, 3)
    turn_e.wait_recv()
    piece_rows(err_t, me.t)[...] = turned_e[...]
    transpose_pair(err_f, pair_rows)
    swaps = []
    mates_rows = pl.ds(pl.multiple_of((1 - me.xl) * TOK, TOK), TOK)
    for n in range(4):
        both[n] = dot(pair_rows[...], w[:, 256 * n : 256 * n + 256])
        grad_sent[n] = both[n, mates_rows, :].astype(BF16)
        swaps.append(net.copy(grad_sent.at[n], grad_got.at[n], me.at_x()))
        swaps[-1].start()
    ring_g = Ring(net, me, grads, TOK, 256)

    def finish_grads(n):
        at = slice(256 * n, 256 * n + 256)
        swaps[n].wait_recv()
        product = both[n, my_rows, :] + grad_got[n].astype(F32)
        grads[my_block, at] = (product * slope[my_rows, at]).astype(BF16)

    for n in range(4):
        finish_grads(n)
        if n < 2:
            ring_g.start(n)
    gather_et = Gather(net, me, err_t, me.by_device)
    gather_et.start()
    ring_c.tick(0, 4)
    ring_c.tick(1, 4)
    ring_g.tick(0, 1)
    ring_g.tick(1, 1)

    def side_by_side(src, dst):
        for f in range(2):
            for z in range(8):
                at = (f * 8 + (z + 1) % 8) * WIDTH
                dst[f, :, z * TOK : (z + 1) * TOK] = src[at : at + WIDTH, :]

    side_by_side(sae_t, left_s)
    ring_g.tick(0, 2)
    ring_g.tick(1, 2)
    ring_g.start(2)
    gather_et.finish()
    ring_g.tick(0, 3)
    ring_g.tick(1, 3)
    ring_g.start(3)
    side_by_side(err_t, left_e)

    def error_term(n):
        for f in range(2):
            at = slice(256 * n, 256 * n + 256)
            wg[f, :, at] = dot(left_e[f], codes[:, at])

    error_term(0)
    error_term(1)

    grad_scale = 1.0 / math.sqrt(TOKENS)
    ones = jnp.ones((8, 8 * TOK), BF16)
    swaps = []

    def finish_columns(n):
        at = slice(256 * n, 256 * n + 256)
        mates = 1 - me.xl
        table = grads[:, at]
        theirs = wg[mates, :, at] + dot(left_s[mates], table)
        wg_sent[n] = (theirs * grad_scale).astype(BF16)
        swaps.append(net.copy(wg_sent.at[n], wg_got.at[n], me.at_x()))
        swaps[-1].start()
        wg[me.xl, :, at] += dot(left_s[me.xl], table)
        bg_here[:, at] = dot(ones, table)

    def save_columns(n):
        at = slice(256 * n, 256 * n + 256)
        swaps[n].wait_recv()
        final[:, at] = (wg[me.xl, :, at] * grad_scale + wg_got[n].astype(F32)).astype(BF16)

    ring_g.tick(2, 1)
    ring_g.tick(0, 4)
    finish_columns(0)
    ring_g.tick(3, 1)
    ring_g.tick(1, 4)
    ring_g.tick(2, 2)
    finish_columns(1)
    ring_g.tick(3, 2)
    error_term(2)
    ring_g.tick(2, 3)
    error_term(3)
    ring_g.tick(3, 3)
    save_columns(0)
    ring_g.tick(2, 4)
    finish_columns(2)
    ring_g.tick(3, 4)
    finish_columns(3)
    bias_swap = net.copy(bg_here, bg_there, me.at_x())
    bias_swap.start()
    save_columns(1)
    save_columns(2)
    save_columns(3)
    save_wg = pltpu.make_async_copy(final, wg_out, local_sem.at[6])
    save_wg.start()
    bias_swap.wait_recv()
    bg[...] = grad_scale * (bg_here[0:1, :] + bg_there[0:1, :])
    save_bg = pltpu.make_async_copy(bg, bg_out, local_sem.at[7])
    save_bg.start()
    net.close()
    save_codes.wait()
    save_wg.wait()
    save_bg.wait()


def local(
    residual,
    segments,
    row_perm,
    pre_gain,
    post_gain,
    w_query,
    w_key,
    w_value,
    w_out,
    sae_weight,
    enc_bias,
    thresholds,
    dec_bias,
):
    vmem = pl.BlockSpec(memory_space=pltpu.VMEM)
    hbm = pl.BlockSpec(memory_space=pl.ANY)
    piece = (WIDTH, TOK)
    whole = (D, TOK)
    wg, bg, codes = pl.pallas_call(
        body,
        out_shape=(
            jax.ShapeDtypeStruct((WIDTH, LANES), BF16),
            jax.ShapeDtypeStruct((1, LANES), F32),
            jax.ShapeDtypeStruct((TOK, LANES), BF16),
        ),
        in_specs=[vmem] * 5 + [hbm] * 5 + [vmem] * 3,
        out_specs=(hbm, hbm, hbm),
        scratch_shapes=[
            pltpu.VMEM((D, 256), BF16),
            pltpu.VMEM((D, 128), BF16),
            pltpu.VMEM((D, 128), BF16),
            pltpu.VMEM((256, D), BF16),
            pltpu.VMEM((HALF, LANES), BF16),
            pltpu.VMEM((3 * TOK, TOK), F32),
            pltpu.VMEM((3 * TOK, TOK), F32),
            pltpu.VMEM(whole, BF16),
            pltpu.VMEM((TOK, D), BF16),
            pltpu.VMEM(whole, BF16),
            pltpu.VMEM((8, *piece), BF16),
            pltpu.VMEM((8, *piece), BF16),
            pltpu.VMEM((8, *piece), BF16),
            pltpu.VMEM(whole, BF16),
            pltpu.VMEM((8, *piece), BF16),
            pltpu.VMEM((8, *piece), BF16),
            pltpu.VMEM((8, *piece), BF16),
            pltpu.VMEM((TOK, TOK), jnp.int32),
            pltpu.VMEM((TOK, TOK), F32),
            pltpu.VMEM((GROUPS, 16, 256), BF16),
            pltpu.VMEM((GROUPS, 16, 256), BF16),
            pltpu.VMEM(whole, BF16),
            pltpu.VMEM(whole, BF16),
            pltpu.VMEM(piece, BF16),
            pltpu.VMEM(piece, BF16),
            pltpu.VMEM(piece, BF16),
            pltpu.VMEM(piece, BF16),
            pltpu.VMEM(whole, BF16),
            pltpu.VMEM(whole, BF16),
            pltpu.VMEM((PAIR, HALF), BF16),
            pltpu.VMEM((4, PAIR, 256), BF16),
            pltpu.VMEM((4, PAIR, 256), BF16),
            pltpu.VMEM((PAIR, LANES), F32),
            pltpu.VMEM((PAIR, LANES), BF16),
            pltpu.VMEM((4, PAIR, 256), F32),
            pltpu.VMEM((4, TOK, 256), BF16),
            pltpu.VMEM((4, TOK, 256), BF16),
            pltpu.VMEM((8 * TOK, LANES), BF16),
            pltpu.VMEM((8 * TOK, LANES), BF16),
            pltpu.VMEM((2, WIDTH, 8 * TOK), BF16),
            pltpu.VMEM((2, WIDTH, 8 * TOK), BF16),
            pltpu.VMEM((2, WIDTH, LANES), F32),
            pltpu.VMEM((4, WIDTH, 256), BF16),
            pltpu.VMEM((4, WIDTH, 256), BF16),
            pltpu.VMEM((WIDTH, LANES), BF16),
            pltpu.VMEM((8, LANES), F32),
            pltpu.VMEM((8, LANES), F32),
            pltpu.VMEM((1, LANES), F32),
            pltpu.SemaphoreType.DMA((8,)),
            pltpu.SemaphoreType.DMA((SEMS,)),
            pltpu.SemaphoreType.DMA((SEMS,)),
        ],
        compiler_params=pltpu.CompilerParams(
            collective_id=0, has_side_effects=True, vmem_limit_bytes=60 * 1024 * 1024
        ),
    )(
        residual.T,
        segments,
        row_perm.reshape(1, TOK),
        pre_gain.reshape(D // TOK, TOK),
        post_gain.reshape(D // TOK, TOK),
        w_query,
        w_key,
        w_value,
        w_out,
        sae_weight,
        enc_bias.reshape(1, LANES),
        thresholds.reshape(1, LANES),
        dec_bias.reshape(D // TOK, TOK),
    )
    return wg, bg.reshape(LANES), codes


def solution(mesh):
    features = ("tensor", "latent")
    return jax.shard_map(
        local,
        mesh=mesh,
        in_specs=(
            P("dp", features),
            P("dp", None),
            P("dp"),
            P(),
            P(),
            P(None, features),
            P(None, features),
            P(None, features),
            P(features, None),
            P("dp", features),
            P(features),
            P(features),
            P(),
        ),
        out_specs=(P("dp", features), P(features), P("dp", features)),
        check_vma=False,
    )
```

```python
import math

import jax
import jax.numpy as jnp
from jax import lax
from jax.experimental import pallas as pl
from jax.experimental.pallas import tpu as pltpu
from jax.sharding import PartitionSpec as P

D = 4608
HEADS = 32
HEAD = 128
LANES = 1024
TOK = 128
GROUPS = 16
TOKENS = TOK * GROUPS
BLOCK = 8
WIDTH = D // 16
HALF = D // 2
PAIR = 2 * TOK
SEMS = 300

epsilon = 1e-06
softcap = 50.0
ramp_width = 0.05
rotary_base = 10000.0

MESH = pl.DeviceIdType.MESH
F32 = jnp.float32
BF16 = jnp.bfloat16
ROW_BY_ROW = (((1,), (1,)), ((), ()))


def dot(a, b):
    return jnp.dot(a, b, preferred_element_type=F32)


def dot_t(a, b):
    return lax.dot_general(a, b, ROW_BY_ROW, preferred_element_type=F32)


class Place:
    def __init__(self):
        self.dp = lax.axis_index("dp")
        self.ten = lax.axis_index("tensor")
        self.lat = lax.axis_index("latent")
        self.xl, self.z = self.dp // 8, self.dp % 8
        self.xh, self.core = self.ten // 2, self.ten % 2
        self.t = self.ten * 4 + self.lat
        self.eighth = self.core * 4 + self.lat
        self.half = (self.xl + self.xh) % 2
        self.group = (self.xl + self.xh + 1) % 2

    def at(self, dp=None, ten=None, lat=None):
        return {
            "dp": self.dp if dp is None else dp,
            "tensor": self.ten if ten is None else ten,
            "latent": self.lat if lat is None else lat,
        }

    def at_x(self):
        return self.at(dp=(1 - self.xl) * 8 + self.z)

    def chip(self, k, sign=1):
        return (self.xh + k // 4) % 2, (self.lat + sign * (k % 4) + 4) % 4

    def by_device(self, k, core, sign=1):
        xh, y = self.chip(k, sign)
        return (xh * 2 + core) * 4 + y

    def by_half(self, k, core, sign=1):
        xh, y = self.chip(k, sign)
        return (((self.xl + xh) % 2) * 2 + core) * 4 + y

    def by_group(self, k, core, sign=1):
        xh, y = self.chip(k, sign)
        return (((self.xl + xh + 1) % 2) * 2 + core) * 4 + y

    def peer(self, k, core=None):
        xh, y = self.chip(k)
        return self.at(ten=xh * 2 + (self.core if core is None else core), lat=y)

    def sibling(self):
        return self.at(ten=self.xh * 2 + 1 - self.core)


class Net:
    def __init__(self, send, recv):
        self.send, self.recv, self.used, self.open = send, recv, 0, []

    def copy(self, src, dst, device):
        i = self.used
        self.used += 1
        assert i < SEMS
        c = pltpu.make_async_remote_copy(
            src_ref=src,
            dst_ref=dst,
            send_sem=self.send.at[i],
            recv_sem=self.recv.at[i],
            device_id=device,
            device_id_type=MESH,
        )
        self.open.append(c)
        return c

    def close(self):
        for c in self.open:
            c.wait_send()
        self.open = []


FAR_FIRST = (6, 5, 7, 4, 2, 1, 3)
NEAR_FIRST = (1, 3, 2, 4, 5, 7, 6)


def piece_rows(ref, index):
    return ref.at[pl.ds(pl.multiple_of(index * WIDTH, 32), WIDTH)]


class Gather:
    def __init__(self, net, me, buf, piece):
        self.net, self.me, self.buf, self.piece = net, me, buf, piece

    def send(self, k, device):
        ref = piece_rows(self.buf, self.piece(k, self.me.core, -1))
        c = self.net.copy(ref, ref, device)
        c.start()
        return c

    def start(self):
        me = self.me
        self.first = {k: self.send(0, me.peer(k)) for k in (4, 2, 1, 3)}
        self.near = {0: self.send(0, me.sibling())}

    def finish(self):
        me = self.me
        self.first[4].wait_recv()
        second = {k: self.send(4, me.peer(k)) for k in (2, 1, 3)}
        self.near[4] = self.send(4, me.sibling())
        for k in (1, 3, 2):
            self.first[k].wait_recv()
            self.near[k] = self.send(k, me.sibling())
        for k in (1, 3, 2):
            second[k].wait_recv()
            self.near[4 + k] = self.send(4 + k, me.sibling())
        for c in self.near.values():
            c.wait_recv()


def reduce_to_owner(net, me, piece, part, mate, out, got):
    order = (*FAR_FIRST, 0)
    pair = {}
    for k in order:
        pair[k] = net.copy(piece_rows(part, piece(k, 1 - me.core)), mate.at[k], me.sibling())
        pair[k].start()
    away = {}
    for k in order:
        pair[k].wait_recv()
        both = piece_rows(part, piece(k, me.core))[...].astype(F32) + mate[k].astype(F32)
        if k == 0:
            total = both
        else:
            out[k] = both.astype(BF16)
            away[k] = net.copy(out.at[k], got.at[k], me.peer(k))
            away[k].start()
    for k in NEAR_FIRST:
        away[k].wait_recv()
        total = total + got[k].astype(F32)
    return total


class Ring:
    def __init__(self, net, me, buf, size, width):
        self.net, self.me, self.buf, self.size, self.width = net, me, buf, size, width
        self.moves = {}

    def move(self, chunk, sign, step):
        me = self.me
        lo, count = 0, self.size
        if step == 4:
            count = self.size // 2
            lo = 0 if sign > 0 else count
        block = (me.z - sign * (step - 1) + 8) % 8
        ref = self.buf.at[
            pl.ds(pl.multiple_of(block * self.size + lo, 16), count),
            pl.ds(chunk * self.width, self.width),
        ]
        c = self.net.copy(ref, ref, me.at(dp=me.xl * 8 + (me.z + sign + 8) % 8))
        c.start()
        self.moves[chunk, sign, step] = c

    def start(self, chunk):
        for sign in (1, -1):
            self.move(chunk, sign, 1)

    def tick(self, chunk, step):
        for sign in (1, -1):
            self.moves[chunk, sign, step].wait_recv()
            if step < 4:
                self.move(chunk, sign, step + 1)


def spread(vec, piece, col):
    for i in range(3):
        row = vec[pl.ds(piece * 9 // 4 + i, 1), :]
        col[i * TOK : (i + 1) * TOK, :] = jnp.broadcast_to(row, (TOK, TOK)).T
    return pl.ds(pl.multiple_of(piece % 4 * 32, 32), WIDTH)


def transpose_into(src, dst, count):
    @pl.loop(0, count)
    def _(i):
        at = pl.multiple_of(i * TOK, TOK)
        dst[:, pl.ds(at, TOK)] = src[pl.ds(at, TOK), :].T


def transpose_pair(src, dst):
    @pl.loop(0, HALF // TOK)
    def _(i):
        at = pl.multiple_of(i * TOK, TOK)
        dst[:TOK, pl.ds(at, TOK)] = src[pl.ds(at, TOK), :].T
        dst[TOK:, pl.ds(at, TOK)] = src[pl.ds(HALF + at, TOK), :].T


def body(
    res,
    seg,
    perm,
    pre_gain,
    post_gain,
    wq_hbm,
    wk_hbm,
    wv_hbm,
    wo_hbm,
    w_hbm,
    enc_bias,
    thr,
    dec_bias,
    wg_out,
    bg_out,
    codes_out,
    wq,
    wk,
    wv,
    wo,
    w,
    gain_col,
    bias_col,
    feat,
    rows,
    part,
    mate,
    out,
    got,
    part2,
    mate2,
    out2,
    got2,
    asked,
    squares,
    sent,
    taken,
    sae_f,
    err_f,
    sae_mine,
    err_mine,
    turned_s,
    turned_e,
    sae_t,
    err_t,
    pair_rows,
    acts_here,
    acts_there,
    slope,
    codes2,
    both,
    grad_sent,
    grad_got,
    codes,
    grads,
    left_s,
    left_e,
    wg,
    wg_sent,
    wg_got,
    final,
    bg_here,
    bg_there,
    bg,
    local_sem,
    send_sem,
    recv_sem,
):
    me = Place()
    net = Net(send_sem, recv_sem)

    loads = []
    for i, (src, dst) in enumerate(
        [
            (w_hbm, piece_rows(w, me.z)),
            (wq_hbm, wq),
            (wk_hbm, wk),
            (wv_hbm, wv),
            (wo_hbm, wo),
        ]
    ):
        loads.append(pltpu.make_async_copy(src, dst, local_sem.at[i]))
        loads[-1].start()

    turn = (me.z + 1) % 8
    turn_to = me.at(dp=me.group * 8 + me.eighth, ten=me.xl * 2 + turn // 4, lat=turn % 4)
    turn_from = me.at(dp=me.xh * 8 + (me.eighth + 7) % 8, ten=me.group * 2 + me.z // 4, lat=me.z % 4)

    greeted = [turn_from, me.sibling()]
    for k in range(1, 8):
        for core in range(2):
            greeted.append(me.peer(k, core))

    def dp_peer(j):
        return ((me.xl + j // 8) % 2) * 8 + (me.z + j % 8) % 8

    for j in range(1, 16):
        greeted.append(me.at(dp=dp_peer(j)))
    for j in range(16):
        if j != 8:
            x = (me.group + j // 8) % 2
            z = (me.z + 8 - j % 8) % 8
            greeted.append(me.at(dp=x * 8 + z, ten=((x + me.xl) % 2) * 2 + me.core))
    barrier = pltpu.get_barrier_semaphore()
    for device in greeted:
        pl.semaphore_signal(barrier, inc=1, device_id=device, device_id_type=MESH)

    @pl.when(me.xh == 1)
    def _():
        pl.semaphore_signal(barrier, inc=1, device_id=me.at_x(), device_id_type=MESH)

    pl.semaphore_wait(barrier, len(greeted) + me.xh)

    piece_rows(feat, me.t)[...] = res[...]
    gather = Gather(net, me, feat, me.by_device)
    gather.start()

    def eight_rows(ref, index):
        return ref.at[pl.ds(pl.multiple_of(index * 8, 8), 8)]

    eight_rows(asked, me.dp)[...] = jnp.broadcast_to(perm[...], (8, TOK))
    asks = []
    for j in range(1, 16):
        own = eight_rows(asked, me.dp)
        asks.append(net.copy(own, own, me.at(dp=dp_peer(j))))
        asks[-1].start()

    loads[0].wait()
    ring = Ring(net, me, w, WIDTH, 512)
    ring.start(0)
    ring.start(1)

    lane = lax.broadcasted_iota(jnp.int32, (TOK, TOK), 1)
    row = lax.broadcasted_iota(jnp.int32, (TOK, TOK), 0)
    seg_k = jnp.broadcast_to(seg[...].astype(F32), (TOK, TOK))
    same = seg_k == seg_k.T
    position = jnp.sum(jnp.where(same & (lane < row), 1.0, 0.0), axis=1, keepdims=True)
    allowed = same & (lane <= row)
    step = (lane % 64).astype(F32)
    angle = position * jnp.exp(step * (-2.0 / HEAD * math.log(rotary_base)))
    cosine = jnp.cos(angle)
    sine = jnp.sin(angle)
    sine = jnp.where(lane < 64, -sine, sine)

    gain_at = spread(post_gain, me.half * 8 + me.eighth, gain_col)
    bias_at = spread(dec_bias, me.xl * 8 + me.eighth, bias_col)

    for c in asks:
        c.wait_recv()
    place = 8 * me.dp + row % 8
    mine = jnp.where(lane == place, asked[...], 0).astype(F32)
    number = jnp.sum(mine, axis=1, keepdims=True) - (me.dp * TOK).astype(F32)
    pick = jnp.where(number == lane.astype(F32), 1.0, 0.0).astype(BF16)

    gather.finish()
    ring.tick(0, 1)
    transpose_into(feat, rows, D // TOK)

    def add_squares(i, acc):
        x = rows[:, pl.ds(pl.multiple_of(i * TOK, TOK), TOK)].astype(F32)
        return acc + x * x

    acc = lax.fori_loop(0, D // TOK, add_squares, jnp.zeros((TOK, TOK), F32), unroll=4)
    scale = lax.rsqrt(jnp.sum(acc, axis=1, keepdims=True) * (1.0 / D) + epsilon)

    @pl.loop(0, D // TOK, unroll=4)
    def _(i):
        at = pl.ds(pl.multiple_of(i * TOK, TOK), TOK)
        rows[:, at] = (rows[:, at].astype(F32) * scale * pre_gain[pl.ds(i, 1), :]).astype(BF16)

    for c in loads[1:]:
        c.wait()
    normed = rows[...]
    query = dot(normed, wq[...])
    key = dot(normed, wk[...])
    value = dot(normed, wv[...]).astype(BF16)

    def rotate(v):
        return (v * cosine + pltpu.roll(v, 64, 1) * sine).astype(BF16)

    key = rotate(key)
    heads = []
    for h in range(2):
        q = rotate(query[:, h * HEAD : (h + 1) * HEAD])
        scores = dot_t(q, key) * (D / HEADS) ** (-0.5)
        scores = softcap * jnp.tanh(scores / softcap)
        weighted = jnp.where(allowed, jnp.exp(scores), 0.0)
        probs = (weighted / jnp.sum(weighted, axis=1, keepdims=True)).astype(BF16)
        heads.append(dot(probs, value).astype(BF16))
    heads = jnp.concatenate(heads, axis=1)

    ring.tick(1, 1)

    @pl.loop(0, D // 256)
    def _(i):
        at = pl.multiple_of(i * 256, 256)
        part[pl.ds(at, 256), :] = dot(heads, wo[:, pl.ds(at, 256)]).astype(BF16).T

    attn = reduce_to_owner(net, me, me.by_half, part, mate, out, got)

    total = jnp.sum(attn * attn, axis=0, keepdims=True)
    own = eight_rows(squares, me.t)
    own[...] = jnp.broadcast_to(total, (8, TOK))
    sums = []
    for k in range(8):
        for core in range(2):
            if k or core:
                device = me.peer(k, (me.core + core) % 2)
                sums.append(net.copy(own, own, device))
                sums[-1].start()
    ring.tick(0, 2)
    for c in sums:
        c.wait_recv()
    ring.tick(1, 2)
    total = jnp.sum(squares[...], axis=0, keepdims=True) * (0.125 / D)
    stream = piece_rows(feat, me.half * 8 + me.eighth)[...].astype(F32)
    hidden = stream + attn * lax.rsqrt(total + epsilon) * gain_col[gain_at, :]
    hidden = hidden.astype(BF16)

    low = dot_t(pick, hidden[:256])
    high = dot_t(pick, hidden[32:])
    for g in range(GROUPS):
        block = jnp.concatenate([low[8 * g : 8 * g + 8], high[8 * g : 8 * g + 8]], axis=0)
        sent[g] = block.astype(BF16)
    moves = []
    to = dp_peer(8)
    other = net.copy(sent.at[to], taken.at[me.dp], me.at_x())
    net.open.pop()

    @pl.when(me.xh == 1)
    def _():
        other.start()

    @pl.when(me.xh == 0)
    def _():
        taken[me.dp] = sent[to]

    for j in (15, 14, 13, 12, 11, 10, 9, 4, 3, 5, 2, 6, 1, 7, 0):
        to = dp_peer(j)
        x, z = to // 8, to % 8
        ten = ((x + me.half + 1) % 2) * 2 + me.core
        moves.append(net.copy(sent.at[to], taken.at[me.dp], me.at(dp=me.half * 8 + z, ten=ten)))
        moves[-1].start()

    @pl.when(me.xh == 1)
    def _():
        other.wait()

    for c in moves:
        c.wait_recv()
    low, high = [], []
    for g in range(GROUPS):
        block = taken[g].astype(F32)
        low.append(block[:8])
        high.append(block[8:, 128:])
    low = jnp.concatenate(low, axis=0)
    high = jnp.concatenate(high, axis=0)
    sae_mine[...] = jnp.concatenate([low.T, high.T[96:]], axis=0).astype(BF16)
    piece_rows(sae_f, me.group * 8 + me.eighth)[...] = sae_mine[...]
    gather = Gather(net, me, sae_f, me.by_group)
    gather.start()
    ring.tick(0, 3)
    ring.tick(1, 3)
    gather.finish()
    turn_s = net.copy(sae_mine, turned_s, turn_to)
    turn_s.start()
    transpose_pair(sae_f, pair_rows)
    ring.tick(0, 4)
    ring.tick(1, 4)

    swaps = []
    for n in range(4):
        at = slice(256 * n, 256 * n + 256)
        acts_here[n] = dot(pair_rows[...], w[:, at]).astype(BF16)
        swaps.append(net.copy(acts_here.at[n], acts_there.at[n], me.at_x()))
        swaps[-1].start()
    turn_s.wait_recv()
    piece_rows(sae_t, me.t)[...] = turned_s[...]
    gather_st = Gather(net, me, sae_t, me.by_device)
    gather_st.start()
    for n in range(4):
        at = slice(256 * n, 256 * n + 256)
        swaps[n].wait_recv()
        acts = acts_here[n].astype(F32) + acts_there[n].astype(F32) + enc_bias[:, at]
        opened = jax.nn.sigmoid((acts - thr[:, at]) / ramp_width)
        slope[:, at] = opened + acts * opened * (1.0 - opened) / ramp_width
        codes2[:, at] = (acts * opened).astype(BF16)
    my_rows = pl.ds(pl.multiple_of(me.xl * TOK, TOK), TOK)
    my_block = pl.ds(pl.multiple_of(me.z * TOK, TOK), TOK)
    codes[my_block, :] = codes2[my_rows, :]
    ring_c = Ring(net, me, codes, TOK, 512)
    ring_c.start(0)
    ring_c.start(1)
    save_codes = pltpu.make_async_copy(codes.at[my_block], codes_out, local_sem.at[5])
    save_codes.start()
    mine = codes2[...]

    @pl.loop(0, 8)
    def _(i):
        at = pl.ds(pl.multiple_of(i * WIDTH, 32), WIDTH)
        rebuilt = dot_t(w[at, :], mine).astype(BF16)
        part2[at, :] = rebuilt[:, :TOK]
        part2[pl.ds(pl.multiple_of(HALF + i * WIDTH, 32), WIDTH), :] = rebuilt[:, TOK:]

    gather_st.finish()
    ring_c.tick(0, 1)
    ring_c.tick(1, 1)
    rebuilt = reduce_to_owner(net, me, me.by_group, part2, mate2, out2, got2)
    error = (rebuilt + bias_col[bias_at, :] - sae_mine[...].astype(F32)).astype(BF16)
    err_mine[...] = error
    piece_rows(err_f, me.group * 8 + me.eighth)[...] = error
    gather = Gather(net, me, err_f, me.by_group)
    gather.start()
    turn_e = net.copy(err_mine, turned_e, turn_to)
    turn_e.start()
    ring_c.tick(0, 2)
    ring_c.tick(1, 2)
    gather.finish()
    ring_c.tick(0, 3)
    ring_c.tick(1, 3)
    turn_e.wait_recv()
    piece_rows(err_t, me.t)[...] = turned_e[...]
    transpose_pair(err_f, pair_rows)
    swaps = []
    mates_rows = pl.ds(pl.multiple_of((1 - me.xl) * TOK, TOK), TOK)
    for n in range(4):
        both[n] = dot(pair_rows[...], w[:, 256 * n : 256 * n + 256])
        grad_sent[n] = both[n, mates_rows, :].astype(BF16)
        swaps.append(net.copy(grad_sent.at[n], grad_got.at[n], me.at_x()))
        swaps[-1].start()
    ring_g = Ring(net, me, grads, TOK, 256)

    def finish_grads(n):
        at = slice(256 * n, 256 * n + 256)
        swaps[n].wait_recv()
        product = both[n, my_rows, :] + grad_got[n].astype(F32)
        grads[my_block, at] = (product * slope[my_rows, at]).astype(BF16)

    for n in range(4):
        finish_grads(n)
        ring_g.start(n)
    gather_et = Gather(net, me, err_t, me.by_device)
    gather_et.start()
    ring_c.tick(0, 4)
    ring_c.tick(1, 4)
    for n in range(4):
        ring_g.tick(n, 1)

    def side_by_side(src, dst):
        for f in range(2):
            for z in range(8):
                at = (f * 8 + (z + 1) % 8) * WIDTH
                dst[f, :, z * TOK : (z + 1) * TOK] = src[at : at + WIDTH, :]

    side_by_side(sae_t, left_s)
    gather_et.finish()
    ring_g.tick(0, 2)
    ring_g.tick(1, 2)
    ring_g.tick(2, 2)
    side_by_side(err_t, left_e)

    def error_term(n):
        for f in range(2):
            at = slice(256 * n, 256 * n + 256)
            wg[f, :, at] = dot(left_e[f], codes[:, at])

    error_term(0)
    ring_g.tick(0, 3)
    ring_g.tick(1, 3)
    ring_g.tick(3, 2)
    error_term(1)

    grad_scale = 1.0 / math.sqrt(TOKENS)
    ones = jnp.ones((8, 8 * TOK), BF16)
    swaps = []

    def finish_columns(n):
        at = slice(256 * n, 256 * n + 256)
        mates = 1 - me.xl
        table = grads[:, at]
        theirs = wg[mates, :, at] + dot(left_s[mates], table)
        wg_sent[n] = (theirs * grad_scale).astype(BF16)
        swaps.append(net.copy(wg_sent.at[n], wg_got.at[n], me.at_x()))
        swaps[-1].start()
        wg[me.xl, :, at] += dot(left_s[me.xl], table)
        bg_here[:, at] = dot(ones, table)

    def save_columns(n):
        at = slice(256 * n, 256 * n + 256)
        swaps[n].wait_recv()
        final[:, at] = (wg[me.xl, :, at] * grad_scale + wg_got[n].astype(F32)).astype(BF16)

    ring_g.tick(0, 4)
    finish_columns(0)
    ring_g.tick(2, 3)
    ring_g.tick(1, 4)
    finish_columns(1)
    ring_g.tick(3, 3)
    error_term(2)
    error_term(3)
    save_columns(0)
    ring_g.tick(2, 4)
    finish_columns(2)
    ring_g.tick(3, 4)
    finish_columns(3)
    bias_swap = net.copy(bg_here, bg_there, me.at_x())
    bias_swap.start()
    save_columns(1)
    save_columns(2)
    save_columns(3)
    save_wg = pltpu.make_async_copy(final, wg_out, local_sem.at[6])
    save_wg.start()
    bias_swap.wait_recv()
    bg[...] = grad_scale * (bg_here[0:1, :] + bg_there[0:1, :])
    save_bg = pltpu.make_async_copy(bg, bg_out, local_sem.at[7])
    save_bg.start()
    net.close()
    save_codes.wait()
    save_wg.wait()
    save_bg.wait()


def local(
    residual,
    segments,
    row_perm,
    pre_gain,
    post_gain,
    w_query,
    w_key,
    w_value,
    w_out,
    sae_weight,
    enc_bias,
    thresholds,
    dec_bias,
):
    vmem = pl.BlockSpec(memory_space=pltpu.VMEM)
    hbm = pl.BlockSpec(memory_space=pl.ANY)
    piece = (WIDTH, TOK)
    whole = (D, TOK)
    wg, bg, codes = pl.pallas_call(
        body,
        out_shape=(
            jax.ShapeDtypeStruct((WIDTH, LANES), BF16),
            jax.ShapeDtypeStruct((1, LANES), F32),
            jax.ShapeDtypeStruct((TOK, LANES), BF16),
        ),
        in_specs=[vmem] * 5 + [hbm] * 5 + [vmem] * 3,
        out_specs=(hbm, hbm, hbm),
        scratch_shapes=[
            pltpu.VMEM((D, 256), BF16),
            pltpu.VMEM((D, 128), BF16),
            pltpu.VMEM((D, 128), BF16),
            pltpu.VMEM((256, D), BF16),
            pltpu.VMEM((HALF, LANES), BF16),
            pltpu.VMEM((3 * TOK, TOK), F32),
            pltpu.VMEM((3 * TOK, TOK), F32),
            pltpu.VMEM(whole, BF16),
            pltpu.VMEM((TOK, D), BF16),
            pltpu.VMEM(whole, BF16),
            pltpu.VMEM((8, *piece), BF16),
            pltpu.VMEM((8, *piece), BF16),
            pltpu.VMEM((8, *piece), BF16),
            pltpu.VMEM(whole, BF16),
            pltpu.VMEM((8, *piece), BF16),
            pltpu.VMEM((8, *piece), BF16),
            pltpu.VMEM((8, *piece), BF16),
            pltpu.VMEM((TOK, TOK), jnp.int32),
            pltpu.VMEM((TOK, TOK), F32),
            pltpu.VMEM((GROUPS, 16, 256), BF16),
            pltpu.VMEM((GROUPS, 16, 256), BF16),
            pltpu.VMEM(whole, BF16),
            pltpu.VMEM(whole, BF16),
            pltpu.VMEM(piece, BF16),
            pltpu.VMEM(piece, BF16),
            pltpu.VMEM(piece, BF16),
            pltpu.VMEM(piece, BF16),
            pltpu.VMEM(whole, BF16),
            pltpu.VMEM(whole, BF16),
            pltpu.VMEM((PAIR, HALF), BF16),
            pltpu.VMEM((4, PAIR, 256), BF16),
            pltpu.VMEM((4, PAIR, 256), BF16),
            pltpu.VMEM((PAIR, LANES), F32),
            pltpu.VMEM((PAIR, LANES), BF16),
            pltpu.VMEM((4, PAIR, 256), F32),
            pltpu.VMEM((4, TOK, 256), BF16),
            pltpu.VMEM((4, TOK, 256), BF16),
            pltpu.VMEM((8 * TOK, LANES), BF16),
            pltpu.VMEM((8 * TOK, LANES), BF16),
            pltpu.VMEM((2, WIDTH, 8 * TOK), BF16),
            pltpu.VMEM((2, WIDTH, 8 * TOK), BF16),
            pltpu.VMEM((2, WIDTH, LANES), F32),
            pltpu.VMEM((4, WIDTH, 256), BF16),
            pltpu.VMEM((4, WIDTH, 256), BF16),
            pltpu.VMEM((WIDTH, LANES), BF16),
            pltpu.VMEM((8, LANES), F32),
            pltpu.VMEM((8, LANES), F32),
            pltpu.VMEM((1, LANES), F32),
            pltpu.SemaphoreType.DMA((8,)),
            pltpu.SemaphoreType.DMA((SEMS,)),
            pltpu.SemaphoreType.DMA((SEMS,)),
        ],
        compiler_params=pltpu.CompilerParams(
            collective_id=0, has_side_effects=True, vmem_limit_bytes=60 * 1024 * 1024
        ),
    )(
        residual.T,
        segments,
        row_perm.reshape(1, TOK),
        pre_gain.reshape(D // TOK, TOK),
        post_gain.reshape(D // TOK, TOK),
        w_query,
        w_key,
        w_value,
        w_out,
        sae_weight,
        enc_bias.reshape(1, LANES),
        thresholds.reshape(1, LANES),
        dec_bias.reshape(D // TOK, TOK),
    )
    return wg, bg.reshape(LANES), codes


def solution(mesh):
    features = ("tensor", "latent")
    return jax.shard_map(
        local,
        mesh=mesh,
        in_specs=(
            P("dp", features),
            P("dp", None),
            P("dp"),
            P(),
            P(),
            P(None, features),
            P(None, features),
            P(None, features),
            P(features, None),
            P("dp", features),
            P(features),
            P(features),
            P(),
        ),
        out_specs=(P("dp", features), P(features), P("dp", features)),
        check_vma=False,
    )
```

```python
import math

import jax
import jax.numpy as jnp
from jax import lax
from jax.experimental import pallas as pl
from jax.experimental.pallas import tpu as pltpu
from jax.sharding import PartitionSpec as P

D = 4608
HEADS = 32
HEAD = 128
LANES = 1024
TOK = 128
GROUPS = 16
TOKENS = TOK * GROUPS
BLOCK = 8
WIDTH = D // 16
HALF = D // 2
PAIR = 2 * TOK
SEMS = 300

epsilon = 1e-06
softcap = 50.0
ramp_width = 0.05
rotary_base = 10000.0

MESH = pl.DeviceIdType.MESH
F32 = jnp.float32
BF16 = jnp.bfloat16
ROW_BY_ROW = (((1,), (1,)), ((), ()))


def dot(a, b):
    return jnp.dot(a, b, preferred_element_type=F32)


def dot_t(a, b):
    return lax.dot_general(a, b, ROW_BY_ROW, preferred_element_type=F32)


class Place:
    def __init__(self):
        self.dp = lax.axis_index("dp")
        self.ten = lax.axis_index("tensor")
        self.lat = lax.axis_index("latent")
        self.xl, self.z = self.dp // 8, self.dp % 8
        self.xh, self.core = self.ten // 2, self.ten % 2
        self.t = self.ten * 4 + self.lat
        self.eighth = self.core * 4 + self.lat
        self.half = (self.xl + self.xh) % 2
        self.group = (self.xl + self.xh + 1) % 2

    def at(self, dp=None, ten=None, lat=None):
        return {
            "dp": self.dp if dp is None else dp,
            "tensor": self.ten if ten is None else ten,
            "latent": self.lat if lat is None else lat,
        }

    def at_x(self):
        return self.at(dp=(1 - self.xl) * 8 + self.z)

    def chip(self, k, sign=1):
        return (self.xh + k // 4) % 2, (self.lat + sign * (k % 4) + 4) % 4

    def by_device(self, k, core, sign=1):
        xh, y = self.chip(k, sign)
        return (xh * 2 + core) * 4 + y

    def by_half(self, k, core, sign=1):
        xh, y = self.chip(k, sign)
        return (((self.xl + xh) % 2) * 2 + core) * 4 + y

    def by_group(self, k, core, sign=1):
        xh, y = self.chip(k, sign)
        return (((self.xl + xh + 1) % 2) * 2 + core) * 4 + y

    def peer(self, k, core=None):
        xh, y = self.chip(k)
        return self.at(ten=xh * 2 + (self.core if core is None else core), lat=y)

    def sibling(self):
        return self.at(ten=self.xh * 2 + 1 - self.core)


class Net:
    def __init__(self, send, recv):
        self.send, self.recv, self.used, self.open = send, recv, 0, []

    def copy(self, src, dst, device):
        i = self.used
        self.used += 1
        assert i < SEMS
        c = pltpu.make_async_remote_copy(
            src_ref=src,
            dst_ref=dst,
            send_sem=self.send.at[i],
            recv_sem=self.recv.at[i],
            device_id=device,
            device_id_type=MESH,
        )
        self.open.append(c)
        return c

    def close(self):
        for c in self.open:
            c.wait_send()
        self.open = []


FAR_FIRST = (6, 5, 7, 4, 2, 1, 3)
NEAR_FIRST = (1, 3, 2, 4, 5, 7, 6)


def piece_rows(ref, index):
    return ref.at[pl.ds(pl.multiple_of(index * WIDTH, 32), WIDTH)]


class Gather:
    def __init__(self, net, me, buf, piece):
        self.net, self.me, self.buf, self.piece = net, me, buf, piece

    def send(self, k, device):
        ref = piece_rows(self.buf, self.piece(k, self.me.core, -1))
        c = self.net.copy(ref, ref, device)
        c.start()
        return c

    def start(self):
        me = self.me
        self.first = {k: self.send(0, me.peer(k)) for k in (4, 2, 1, 3)}
        self.near = {0: self.send(0, me.sibling())}

    def finish(self):
        me = self.me
        self.first[4].wait_recv()
        second = {k: self.send(4, me.peer(k)) for k in (2, 1, 3)}
        self.near[4] = self.send(4, me.sibling())
        for k in (1, 3, 2):
            self.first[k].wait_recv()
            self.near[k] = self.send(k, me.sibling())
        for k in (1, 3, 2):
            second[k].wait_recv()
            self.near[4 + k] = self.send(4 + k, me.sibling())
        for c in self.near.values():
            c.wait_recv()


def reduce_to_owner(net, me, piece, part, mate, out, got):
    order = (*FAR_FIRST, 0)
    pair = {}
    for k in order:
        pair[k] = net.copy(piece_rows(part, piece(k, 1 - me.core)), mate.at[k], me.sibling())
        pair[k].start()
    away = {}
    for k in order:
        pair[k].wait_recv()
        both = piece_rows(part, piece(k, me.core))[...].astype(F32) + mate[k].astype(F32)
        if k == 0:
            total = both
        else:
            out[k] = both.astype(BF16)
            away[k] = net.copy(out.at[k], got.at[k], me.peer(k))
            away[k].start()
    for k in NEAR_FIRST:
        away[k].wait_recv()
        total = total + got[k].astype(F32)
    return total


class Ring:
    def __init__(self, net, me, buf, size, width):
        self.net, self.me, self.buf, self.size, self.width = net, me, buf, size, width
        self.moves = {}

    def move(self, chunk, sign, step):
        me = self.me
        lo, count = 0, self.size
        if step == 4:
            count = self.size // 2
            lo = 0 if sign > 0 else count
        block = (me.z - sign * (step - 1) + 8) % 8
        ref = self.buf.at[
            pl.ds(pl.multiple_of(block * self.size + lo, 16), count),
            pl.ds(chunk * self.width, self.width),
        ]
        c = self.net.copy(ref, ref, me.at(dp=me.xl * 8 + (me.z + sign + 8) % 8))
        c.start()
        self.moves[chunk, sign, step] = c

    def start(self, chunk):
        for sign in (1, -1):
            self.move(chunk, sign, 1)

    def tick(self, chunk, step):
        for sign in (1, -1):
            self.moves[chunk, sign, step].wait_recv()
            if step < 4:
                self.move(chunk, sign, step + 1)


def spread(vec, piece, col):
    for i in range(3):
        row = vec[pl.ds(piece * 9 // 4 + i, 1), :]
        col[i * TOK : (i + 1) * TOK, :] = jnp.broadcast_to(row, (TOK, TOK)).T
    return pl.ds(pl.multiple_of(piece % 4 * 32, 32), WIDTH)


def transpose_into(src, dst, count):
    @pl.loop(0, count)
    def _(i):
        at = pl.multiple_of(i * TOK, TOK)
        dst[:, pl.ds(at, TOK)] = src[pl.ds(at, TOK), :].T


def transpose_pair(src, dst):
    @pl.loop(0, HALF // TOK)
    def _(i):
        at = pl.multiple_of(i * TOK, TOK)
        dst[:TOK, pl.ds(at, TOK)] = src[pl.ds(at, TOK), :].T
        dst[TOK:, pl.ds(at, TOK)] = src[pl.ds(HALF + at, TOK), :].T


def body(
    res,
    seg,
    perm,
    pre_gain,
    post_gain,
    wq_hbm,
    wk_hbm,
    wv_hbm,
    wo_hbm,
    w_hbm,
    enc_bias,
    thr,
    dec_bias,
    wg_out,
    bg_out,
    codes_out,
    wq,
    wk,
    wv,
    wo,
    w,
    gain_col,
    bias_col,
    feat,
    rows,
    part,
    mate,
    out,
    got,
    part2,
    mate2,
    out2,
    got2,
    asked,
    squares,
    sent,
    taken,
    sae_f,
    err_f,
    sae_mine,
    err_mine,
    turned_s,
    turned_e,
    sae_t,
    err_t,
    pair_rows,
    acts_here,
    acts_there,
    slope,
    codes2,
    both,
    grad_sent,
    grad_got,
    codes,
    grads,
    left_s,
    left_e,
    wg,
    wg_sent,
    wg_got,
    final,
    bg_here,
    bg_there,
    bg,
    local_sem,
    send_sem,
    recv_sem,
):
    me = Place()
    net = Net(send_sem, recv_sem)

    loads = []
    for i, (src, dst) in enumerate(
        [
            (w_hbm, piece_rows(w, me.z)),
            (wq_hbm, wq),
            (wk_hbm, wk),
            (wv_hbm, wv),
            (wo_hbm, wo),
        ]
    ):
        loads.append(pltpu.make_async_copy(src, dst, local_sem.at[i]))
        loads[-1].start()

    turn = (me.z + 1) % 8
    turn_to = me.at(dp=me.group * 8 + me.eighth, ten=me.xl * 2 + turn // 4, lat=turn % 4)
    turn_from = me.at(dp=me.xh * 8 + (me.eighth + 7) % 8, ten=me.group * 2 + me.z // 4, lat=me.z % 4)

    greeted = [turn_from, me.sibling()]
    for k in range(1, 8):
        for core in range(2):
            greeted.append(me.peer(k, core))

    def dp_peer(j):
        return ((me.xl + j // 8) % 2) * 8 + (me.z + j % 8) % 8

    for j in range(1, 16):
        greeted.append(me.at(dp=dp_peer(j)))
    for j in range(16):
        if j != 8:
            x = (me.group + j // 8) % 2
            z = (me.z + 8 - j % 8) % 8
            greeted.append(me.at(dp=x * 8 + z, ten=((x + me.xl) % 2) * 2 + me.core))
    barrier = pltpu.get_barrier_semaphore()
    for device in greeted:
        pl.semaphore_signal(barrier, inc=1, device_id=device, device_id_type=MESH)

    @pl.when(me.xh == 1)
    def _():
        pl.semaphore_signal(barrier, inc=1, device_id=me.at_x(), device_id_type=MESH)

    pl.semaphore_wait(barrier, len(greeted) + me.xh)

    piece_rows(feat, me.t)[...] = res[...]
    gather = Gather(net, me, feat, me.by_device)
    gather.start()

    def eight_rows(ref, index):
        return ref.at[pl.ds(pl.multiple_of(index * 8, 8), 8)]

    eight_rows(asked, me.dp)[...] = jnp.broadcast_to(perm[...], (8, TOK))
    asks = []
    for j in range(1, 16):
        own = eight_rows(asked, me.dp)
        asks.append(net.copy(own, own, me.at(dp=dp_peer(j))))
        asks[-1].start()

    loads[0].wait()
    ring = Ring(net, me, w, WIDTH, 512)
    ring.start(0)
    ring.start(1)

    lane = lax.broadcasted_iota(jnp.int32, (TOK, TOK), 1)
    row = lax.broadcasted_iota(jnp.int32, (TOK, TOK), 0)
    seg_k = jnp.broadcast_to(seg[...].astype(F32), (TOK, TOK))
    same = seg_k == seg_k.T
    position = jnp.sum(jnp.where(same & (lane < row), 1.0, 0.0), axis=1, keepdims=True)
    allowed = same & (lane <= row)
    step = (lane % 64).astype(F32)
    angle = position * jnp.exp(step * (-2.0 / HEAD * math.log(rotary_base)))
    cosine = jnp.cos(angle)
    sine = jnp.sin(angle)
    sine = jnp.where(lane < 64, -sine, sine)

    gain_at = spread(post_gain, me.half * 8 + me.eighth, gain_col)
    bias_at = spread(dec_bias, me.xl * 8 + me.eighth, bias_col)

    for c in asks:
        c.wait_recv()
    place = 8 * me.dp + row % 8
    mine = jnp.where(lane == place, asked[...], 0).astype(F32)
    number = jnp.sum(mine, axis=1, keepdims=True) - (me.dp * TOK).astype(F32)
    pick = jnp.where(number == lane.astype(F32), 1.0, 0.0).astype(BF16)

    gather.finish()
    ring.tick(0, 1)
    transpose_into(feat, rows, D // TOK)

    def add_squares(i, acc):
        x = rows[:, pl.ds(pl.multiple_of(i * TOK, TOK), TOK)].astype(F32)
        return acc + x * x

    acc = lax.fori_loop(0, D // TOK, add_squares, jnp.zeros((TOK, TOK), F32), unroll=4)
    scale = lax.rsqrt(jnp.sum(acc, axis=1, keepdims=True) * (1.0 / D) + epsilon)

    @pl.loop(0, D // TOK, unroll=4)
    def _(i):
        at = pl.ds(pl.multiple_of(i * TOK, TOK), TOK)
        rows[:, at] = (rows[:, at].astype(F32) * scale * pre_gain[pl.ds(i, 1), :]).astype(BF16)

    for c in loads[1:]:
        c.wait()
    normed = rows[...]
    query = dot(normed, wq[...])
    key = dot(normed, wk[...])
    value = dot(normed, wv[...]).astype(BF16)

    def rotate(v):
        return (v * cosine + pltpu.roll(v, 64, 1) * sine).astype(BF16)

    key = rotate(key)
    heads = []
    for h in range(2):
        q = rotate(query[:, h * HEAD : (h + 1) * HEAD])
        scores = dot_t(q, key) * (D / HEADS) ** (-0.5)
        scores = softcap * jnp.tanh(scores / softcap)
        weighted = jnp.where(allowed, jnp.exp(scores), 0.0)
        probs = (weighted / jnp.sum(weighted, axis=1, keepdims=True)).astype(BF16)
        heads.append(dot(probs, value).astype(BF16))
    heads = jnp.concatenate(heads, axis=1)

    ring.tick(1, 1)

    @pl.loop(0, D // 256)
    def _(i):
        at = pl.multiple_of(i * 256, 256)
        part[pl.ds(at, 256), :] = dot(heads, wo[:, pl.ds(at, 256)]).astype(BF16).T

    attn = reduce_to_owner(net, me, me.by_half, part, mate, out, got)

    total = jnp.sum(attn * attn, axis=0, keepdims=True)
    own = eight_rows(squares, me.t)
    own[...] = jnp.broadcast_to(total, (8, TOK))
    sums = []
    for k in range(8):
        for core in range(2):
            if k or core:
                device = me.peer(k, (me.core + core) % 2)
                sums.append(net.copy(own, own, device))
                sums[-1].start()
    ring.tick(0, 2)
    for c in sums:
        c.wait_recv()
    ring.tick(1, 2)
    total = jnp.sum(squares[...], axis=0, keepdims=True) * (0.125 / D)
    stream = piece_rows(feat, me.half * 8 + me.eighth)[...].astype(F32)
    hidden = stream + attn * lax.rsqrt(total + epsilon) * gain_col[gain_at, :]
    hidden = hidden.astype(BF16)

    low = dot_t(pick, hidden[:256])
    high = dot_t(pick, hidden[32:])
    for g in range(GROUPS):
        block = jnp.concatenate([low[8 * g : 8 * g + 8], high[8 * g : 8 * g + 8]], axis=0)
        sent[g] = block.astype(BF16)
    moves = []
    to = dp_peer(8)
    other = net.copy(sent.at[to], taken.at[me.dp], me.at_x())
    net.open.pop()

    @pl.when(me.xh == 1)
    def _():
        other.start()

    @pl.when(me.xh == 0)
    def _():
        taken[me.dp] = sent[to]

    for j in (15, 14, 13, 12, 11, 10, 9, 4, 3, 5, 2, 6, 1, 7, 0):
        to = dp_peer(j)
        x, z = to // 8, to % 8
        ten = ((x + me.half + 1) % 2) * 2 + me.core
        moves.append(net.copy(sent.at[to], taken.at[me.dp], me.at(dp=me.half * 8 + z, ten=ten)))
        moves[-1].start()

    @pl.when(me.xh == 1)
    def _():
        other.wait()

    for c in moves:
        c.wait_recv()
    low, high = [], []
    for g in range(GROUPS):
        block = taken[g].astype(F32)
        low.append(block[:8])
        high.append(block[8:, 128:])
    low = jnp.concatenate(low, axis=0)
    high = jnp.concatenate(high, axis=0)
    sae_mine[...] = jnp.concatenate([low.T, high.T[96:]], axis=0).astype(BF16)
    piece_rows(sae_f, me.group * 8 + me.eighth)[...] = sae_mine[...]
    gather = Gather(net, me, sae_f, me.by_group)
    gather.start()
    ring.tick(0, 3)
    ring.tick(1, 3)
    gather.finish()
    turn_s = net.copy(sae_mine, turned_s, turn_to)
    turn_s.start()
    transpose_pair(sae_f, pair_rows)
    ring.tick(0, 4)
    ring.tick(1, 4)

    swaps = []
    for n in range(4):
        at = slice(256 * n, 256 * n + 256)
        acts_here[n] = dot(pair_rows[...], w[:, at]).astype(BF16)
        swaps.append(net.copy(acts_here.at[n], acts_there.at[n], me.at_x()))
        swaps[-1].start()
    turn_s.wait_recv()
    piece_rows(sae_t, me.t)[...] = turned_s[...]
    gather_st = Gather(net, me, sae_t, me.by_device)
    gather_st.start()
    for n in range(4):
        at = slice(256 * n, 256 * n + 256)
        swaps[n].wait_recv()
        acts = acts_here[n].astype(F32) + acts_there[n].astype(F32) + enc_bias[:, at]
        opened = jax.nn.sigmoid((acts - thr[:, at]) / ramp_width)
        slope[:, at] = opened + acts * opened * (1.0 - opened) / ramp_width
        codes2[:, at] = (acts * opened).astype(BF16)
    my_rows = pl.ds(pl.multiple_of(me.xl * TOK, TOK), TOK)
    my_block = pl.ds(pl.multiple_of(me.z * TOK, TOK), TOK)
    codes[my_block, :] = codes2[my_rows, :]
    ring_c = Ring(net, me, codes, TOK, 512)
    ring_c.start(0)
    ring_c.start(1)
    save_codes = pltpu.make_async_copy(codes.at[my_block], codes_out, local_sem.at[5])
    save_codes.start()
    mine = codes2[...]

    @pl.loop(0, 8)
    def _(i):
        at = pl.ds(pl.multiple_of(i * WIDTH, 32), WIDTH)
        rebuilt = dot_t(w[at, :], mine).astype(BF16)
        part2[at, :] = rebuilt[:, :TOK]
        part2[pl.ds(pl.multiple_of(HALF + i * WIDTH, 32), WIDTH), :] = rebuilt[:, TOK:]

    gather_st.finish()
    ring_c.tick(0, 1)
    ring_c.tick(1, 1)
    rebuilt = reduce_to_owner(net, me, me.by_group, part2, mate2, out2, got2)
    error = (rebuilt + bias_col[bias_at, :] - sae_mine[...].astype(F32)).astype(BF16)
    err_mine[...] = error
    piece_rows(err_f, me.group * 8 + me.eighth)[...] = error
    gather = Gather(net, me, err_f, me.by_group)
    gather.start()
    turn_e = net.copy(err_mine, turned_e, turn_to)
    turn_e.start()
    ring_c.tick(0, 2)
    ring_c.tick(1, 2)
    gather.finish()
    transpose_pair(err_f, pair_rows)
    swaps = []
    mates_rows = pl.ds(pl.multiple_of((1 - me.xl) * TOK, TOK), TOK)
    for n in range(4):
        both[n] = dot(pair_rows[...], w[:, 256 * n : 256 * n + 256])
        grad_sent[n] = both[n, mates_rows, :].astype(BF16)
        swaps.append(net.copy(grad_sent.at[n], grad_got.at[n], me.at_x()))
        swaps[-1].start()
    ring_c.tick(0, 3)
    ring_c.tick(1, 3)
    turn_e.wait_recv()
    piece_rows(err_t, me.t)[...] = turned_e[...]
    gather_et = Gather(net, me, err_t, me.by_device)
    gather_et.start()
    ring_g = Ring(net, me, grads, TOK, 256)

    def finish_grads(n):
        at = slice(256 * n, 256 * n + 256)
        swaps[n].wait_recv()
        product = both[n, my_rows, :] + grad_got[n].astype(F32)
        grads[my_block, at] = (product * slope[my_rows, at]).astype(BF16)

    for n in range(4):
        finish_grads(n)
        if n < 2:
            ring_g.start(n)
    ring_c.tick(0, 4)
    ring_c.tick(1, 4)
    ring_g.tick(0, 1)
    ring_g.tick(1, 1)

    def side_by_side(src, dst):
        for f in range(2):
            for z in range(8):
                at = (f * 8 + (z + 1) % 8) * WIDTH
                dst[f, :, z * TOK : (z + 1) * TOK] = src[at : at + WIDTH, :]

    side_by_side(sae_t, left_s)
    ring_g.tick(0, 2)
    ring_g.tick(1, 2)
    ring_g.start(2)
    gather_et.finish()
    ring_g.tick(0, 3)
    ring_g.tick(1, 3)
    ring_g.start(3)
    side_by_side(err_t, left_e)

    def error_term(n):
        for f in range(2):
            at = slice(256 * n, 256 * n + 256)
            wg[f, :, at] = dot(left_e[f], codes[:, at])

    error_term(0)
    error_term(1)

    grad_scale = 1.0 / math.sqrt(TOKENS)
    ones = jnp.ones((8, 8 * TOK), BF16)
    swaps = []

    def finish_columns(n):
        at = slice(256 * n, 256 * n + 256)
        mates = 1 - me.xl
        table = grads[:, at]
        theirs = wg[mates, :, at] + dot(left_s[mates], table)
        wg_sent[n] = (theirs * grad_scale).astype(BF16)
        swaps.append(net.copy(wg_sent.at[n], wg_got.at[n], me.at_x()))
        swaps[-1].start()
        wg[me.xl, :, at] += dot(left_s[me.xl], table)
        bg_here[:, at] = dot(ones, table)

    def save_columns(n):
        at = slice(256 * n, 256 * n + 256)
        swaps[n].wait_recv()
        final[:, at] = (wg[me.xl, :, at] * grad_scale + wg_got[n].astype(F32)).astype(BF16)

    ring_g.tick(2, 1)
    ring_g.tick(0, 4)
    finish_columns(0)
    ring_g.tick(3, 1)
    ring_g.tick(1, 4)
    ring_g.tick(2, 2)
    finish_columns(1)
    ring_g.tick(3, 2)
    error_term(2)
    ring_g.tick(2, 3)
    error_term(3)
    ring_g.tick(3, 3)
    save_columns(0)
    ring_g.tick(2, 4)
    finish_columns(2)
    ring_g.tick(3, 4)
    finish_columns(3)
    bias_swap = net.copy(bg_here, bg_there, me.at_x())
    bias_swap.start()
    save_columns(1)
    save_columns(2)
    save_columns(3)
    save_wg = pltpu.make_async_copy(final, wg_out, local_sem.at[6])
    save_wg.start()
    bias_swap.wait_recv()
    bg[...] = grad_scale * (bg_here[0:1, :] + bg_there[0:1, :])
    save_bg = pltpu.make_async_copy(bg, bg_out, local_sem.at[7])
    save_bg.start()
    net.close()
    save_codes.wait()
    save_wg.wait()
    save_bg.wait()


def local(
    residual,
    segments,
    row_perm,
    pre_gain,
    post_gain,
    w_query,
    w_key,
    w_value,
    w_out,
    sae_weight,
    enc_bias,
    thresholds,
    dec_bias,
):
    vmem = pl.BlockSpec(memory_space=pltpu.VMEM)
    hbm = pl.BlockSpec(memory_space=pl.ANY)
    piece = (WIDTH, TOK)
    whole = (D, TOK)
    wg, bg, codes = pl.pallas_call(
        body,
        out_shape=(
            jax.ShapeDtypeStruct((WIDTH, LANES), BF16),
            jax.ShapeDtypeStruct((1, LANES), F32),
            jax.ShapeDtypeStruct((TOK, LANES), BF16),
        ),
        in_specs=[vmem] * 5 + [hbm] * 5 + [vmem] * 3,
        out_specs=(hbm, hbm, hbm),
        scratch_shapes=[
            pltpu.VMEM((D, 256), BF16),
            pltpu.VMEM((D, 128), BF16),
            pltpu.VMEM((D, 128), BF16),
            pltpu.VMEM((256, D), BF16),
            pltpu.VMEM((HALF, LANES), BF16),
            pltpu.VMEM((3 * TOK, TOK), F32),
            pltpu.VMEM((3 * TOK, TOK), F32),
            pltpu.VMEM(whole, BF16),
            pltpu.VMEM((TOK, D), BF16),
            pltpu.VMEM(whole, BF16),
            pltpu.VMEM((8, *piece), BF16),
            pltpu.VMEM((8, *piece), BF16),
            pltpu.VMEM((8, *piece), BF16),
            pltpu.VMEM(whole, BF16),
            pltpu.VMEM((8, *piece), BF16),
            pltpu.VMEM((8, *piece), BF16),
            pltpu.VMEM((8, *piece), BF16),
            pltpu.VMEM((TOK, TOK), jnp.int32),
            pltpu.VMEM((TOK, TOK), F32),
            pltpu.VMEM((GROUPS, 16, 256), BF16),
            pltpu.VMEM((GROUPS, 16, 256), BF16),
            pltpu.VMEM(whole, BF16),
            pltpu.VMEM(whole, BF16),
            pltpu.VMEM(piece, BF16),
            pltpu.VMEM(piece, BF16),
            pltpu.VMEM(piece, BF16),
            pltpu.VMEM(piece, BF16),
            pltpu.VMEM(whole, BF16),
            pltpu.VMEM(whole, BF16),
            pltpu.VMEM((PAIR, HALF), BF16),
            pltpu.VMEM((4, PAIR, 256), BF16),
            pltpu.VMEM((4, PAIR, 256), BF16),
            pltpu.VMEM((PAIR, LANES), F32),
            pltpu.VMEM((PAIR, LANES), BF16),
            pltpu.VMEM((4, PAIR, 256), F32),
            pltpu.VMEM((4, TOK, 256), BF16),
            pltpu.VMEM((4, TOK, 256), BF16),
            pltpu.VMEM((8 * TOK, LANES), BF16),
            pltpu.VMEM((8 * TOK, LANES), BF16),
            pltpu.VMEM((2, WIDTH, 8 * TOK), BF16),
            pltpu.VMEM((2, WIDTH, 8 * TOK), BF16),
            pltpu.VMEM((2, WIDTH, LANES), F32),
            pltpu.VMEM((4, WIDTH, 256), BF16),
            pltpu.VMEM((4, WIDTH, 256), BF16),
            pltpu.VMEM((WIDTH, LANES), BF16),
            pltpu.VMEM((8, LANES), F32),
            pltpu.VMEM((8, LANES), F32),
            pltpu.VMEM((1, LANES), F32),
            pltpu.SemaphoreType.DMA((8,)),
            pltpu.SemaphoreType.DMA((SEMS,)),
            pltpu.SemaphoreType.DMA((SEMS,)),
        ],
        compiler_params=pltpu.CompilerParams(
            collective_id=0, has_side_effects=True, vmem_limit_bytes=60 * 1024 * 1024
        ),
    )(
        residual.T,
        segments,
        row_perm.reshape(1, TOK),
        pre_gain.reshape(D // TOK, TOK),
        post_gain.reshape(D // TOK, TOK),
        w_query,
        w_key,
        w_value,
        w_out,
        sae_weight,
        enc_bias.reshape(1, LANES),
        thresholds.reshape(1, LANES),
        dec_bias.reshape(D // TOK, TOK),
    )
    return wg, bg.reshape(LANES), codes


def solution(mesh):
    features = ("tensor", "latent")
    return jax.shard_map(
        local,
        mesh=mesh,
        in_specs=(
            P("dp", features),
            P("dp", None),
            P("dp"),
            P(),
            P(),
            P(None, features),
            P(None, features),
            P(None, features),
            P(features, None),
            P("dp", features),
            P(features),
            P(features),
            P(),
        ),
        out_specs=(P("dp", features), P(features), P("dp", features)),
        check_vma=False,
    )
```
